256 devices in a mesh: src: 8 (over z), dst: 32 (over x, y, core).
Axes of the slice: x: 4, y: 4, z: 8, core: 2. Of those that a mesh axis runs over, the one named last changes fastest.
Arguments:
- src_emb: bfloat16 [65536, 128], P('src'), may hold values from -1.5 to 1.5
- dst_emb: bfloat16 [65536, 128], P('dst'), may hold values from -1.5 to 1.5
- out_emb: bfloat16 [65536, 128], P('dst'), may hold values from -1.5 to 1.5
- word_table: bfloat16 [32768, 128], P('dst'), may hold values from -1.5 to 1.5
- log_norm: float32 [65536], P('dst'), may hold values from 9 to 11
- block_mask: int32 [128, 128], P('src', 'dst'), may hold values from 0 to 1, as said below
- tokens: int32 [3, 8], replicated, may hold values from 0 to 32767
- alpha_start: float32 [8, 65536], P(None, 'src'), may hold values from 0.5 to 80
- beta_end: float32 [8, 65536], P(None, 'dst'), may hold values from 0.5 to 80
Outputs:
- alpha_end: float32 [8, 65536], P(None, 'dst')
- beta_start: float32 [8, 65536], P(None, 'src')
- block_counts: float32 [128, 128], P('src', 'dst')
The draws below stay inside these ranges and needn't reach their ends.
Inputs may be any that keep to these rules, and one draw needn't show every extreme that they name: block_mask[I, I] = 1 for every block I: a state may always move within its own block.
All inputs are finite; a program needn't handle non-finite values.
Results may differ from the reference program's by a relative error of at most 0.0032.
Values may be sent and summed in bfloat16 or wider, within the bound.
No kernel may reach another device: no remote copies, remote signals or barrier semaphores. Data moves between devices by JAX's collectives and lax.ppermute only.
A program may use at most 128 MiB of HBM per device.

```python
import math
import jax
import jax.numpy as jnp
import numpy as np
from jax import lax

S = 65536
BLK = 512
E = 128
V = 32768
TRACES = 8
STEPS = 3
NB = 128


def draw_src_emb(key, part):
    values = jnp.clip(0.3 * jax.random.normal(jax.random.fold_in(key, 1), (S, E), jnp.float32), -1.5, 1.5)
    return values.astype(jnp.bfloat16)


def draw_dst_emb(key, part):
    values = jnp.clip(0.3 * jax.random.normal(jax.random.fold_in(key, 2), (S, E), jnp.float32), -1.5, 1.5)
    return values.astype(jnp.bfloat16)


def rising_vector(key, salt):
    position = jnp.arange(S, dtype=jnp.float32) / S
    ramp = jnp.exp(jnp.log(10.0) * position)
    rough = jnp.exp(jax.random.uniform(jax.random.fold_in(key, salt), (TRACES, S), jnp.float32, -0.69, 0.69))
    return ramp[None, :] * rough


def draw_alpha_start(key, part):
    return rising_vector(key, 11)


def draw_beta_end(key, part):
    return rising_vector(key, 13)


def draw_block_mask(key, part):
    coin_flips = jax.random.randint(key, (NB, NB), 0, 16)
    rows = jnp.arange(NB)[:, None]
    cols = jnp.arange(NB)[None, :]
    diagonal = rows == cols
    near = jnp.abs(rows - cols) <= NB // 8
    keep = diagonal | near & (coin_flips < 8) | (coin_flips == 0)
    return jnp.where(keep, 1, 0).astype(jnp.int32)


def place_ends(drawn, key, low, largest):
    longest = drawn.shape.index(max(drawn.shape))
    spots = []
    for shift in (0, 1):
        where = [jax.random.randint(jax.random.fold_in(key, axis), (), 0, length) for axis, length in enumerate(drawn.shape)]
        where[longest] = (where[longest] + shift) % drawn.shape[longest]
        spots.append(tuple(where))
    return drawn.at[spots[0]].set(low).at[spots[1]].set(largest)


def block_scale(key, dims, split, low, largest):
    level, own = 1.0, jax.random.fold_in(key, 6)
    for dim, shards_of in split:
        steps = jnp.exp(jax.random.uniform(jax.random.fold_in(own, dim), (shards_of,), jnp.float32, low / len(split), largest / len(split)))
        level = level * jnp.repeat(steps, dims[dim] // shards_of).reshape([-1 if axis == dim else 1 for axis in range(len(dims))])
    return level


def rank_bounds(number_of, slope):
    portions = [(1 << 20) // math.isqrt(grade ** slope) + 1 for grade in range(1, number_of + 1)]
    scale = 1 + sum(portions) // (1 << 30)
    return np.cumsum(np.array([max(1, weight // scale) for weight in portions]))


def ranked(rng, extent, number_of, skew):
    listing = rank_bounds(number_of, skew)
    pick = jax.random.randint(jax.random.fold_in(rng, 1), extent, 0, int(listing[number_of - 1]))
    grade = jnp.searchsorted(jnp.asarray(listing, jnp.int32), pick, side="right")
    return jax.random.permutation(jax.random.fold_in(rng, 2), number_of)[grade].astype(jnp.int32)


def gaussian(key, shape, deviation, most, shards=(), kind=jnp.bfloat16):
    values = deviation * jax.random.normal(key, shape, jnp.float32)
    if shards:
        values = values * block_scale(key, shape, shards, -0.22, 0.18)
    return jnp.clip(values, -most, most).astype(kind)


def setup_inputs(seed: int = 0) -> dict:
    key_of = jax.random.split(jax.random.key(seed), 10)
    src_emb = draw_src_emb(jax.random.fold_in(key_of[9], 71), 0)
    dst_emb = draw_dst_emb(jax.random.fold_in(key_of[9], 71), 0)
    out_emb = gaussian(key_of[2], (S, E), 0.3, 1.5, ((0, 32),))
    word_table = gaussian(key_of[3], (V, E), 0.3, 1.5, ((0, 32),))
    log_norm = jnp.clip(9.0 + 2.0 * jax.random.uniform(key_of[4], (S,), jnp.float32) ** block_scale(key_of[4], (S,), ((0, 32),), -0.2, 0.2), 9.0, 11.0)
    block_mask = draw_block_mask(jax.random.fold_in(key_of[9], 71), 0)
    tokens = place_ends(ranked(key_of[6], (STEPS, TRACES), V, 2), jax.random.fold_in(key_of[6], 3), 0, V - 1).astype(jnp.int32)
    alpha_start = draw_alpha_start(jax.random.fold_in(key_of[9], 71), 0)
    beta_end = draw_beta_end(jax.random.fold_in(key_of[9], 71), 0)
    return dict(src_emb=src_emb, dst_emb=dst_emb, out_emb=out_emb, word_table=word_table, log_norm=log_norm, block_mask=block_mask, tokens=tokens, alpha_start=alpha_start, beta_end=beta_end)


very_negative = -1e30


def block_tables(src_rows, dst_emb, mask_row):
    scores = jnp.dot(src_rows, dst_emb.T, preferred_element_type=jnp.float32)
    scores = scores.reshape(src_rows.shape[0], NB, BLK)
    block_top = jnp.max(scores, axis=2)
    block_sum = jnp.sum(jnp.exp(scores - block_top[:, :, None]), axis=2)
    allowed = (mask_row == 1)[None, :]
    row_best = jnp.max(jnp.where(allowed, block_top, very_negative), axis=1)
    row_mass = jnp.sum(jnp.where(allowed, block_sum * jnp.exp(block_top - row_best[:, None]), 0.0), axis=1)
    log_total = row_best + jnp.log(row_mass)
    factor = jnp.where(allowed, jnp.exp(block_top - log_total[:, None]), 0.0)
    transit = jnp.where(allowed[:, :, None], jnp.exp(scores - block_top[:, :, None]), 0.0).astype(jnp.bfloat16)
    return factor, transit


def sweep(src_emb, dst_emb, block_mask, alphas, weights):
    members = alphas.shape[0]
    traces = alphas.shape[1]
    src_blocks = src_emb.reshape(NB, BLK, E)
    alpha_blocks = alphas.reshape(members, traces, NB, BLK).transpose(2, 0, 1, 3)
    weight_cols = weights.reshape(members, traces, NB, BLK).astype(jnp.float32)

    def one_block(running, inputs):
        src_rows, mask_row, alpha_rows = inputs
        factor, transit = block_tables(src_rows, dst_emb, mask_row)
        transit_wide = transit.astype(jnp.float32)
        mix_terms = (alpha_rows[:, :, :, None] * factor[None, None]).astype(jnp.bfloat16)
        mix_wide = mix_terms.astype(jnp.float32)
        running = running + jnp.einsum("abin,inc->abnc", mix_wide, transit_wide)
        spread = jnp.einsum("inc,abnc->abin", transit_wide, weight_cols)
        partial_value = jnp.sum(factor[None, None] * spread, axis=3)
        block_terms = jnp.sum(mix_wide * spread, axis=2)
        return running, (partial_value, block_terms)

    zeros_start = jnp.zeros((members, traces, NB, BLK), jnp.float32)
    predicted, (partial_value, block_terms) = lax.scan(one_block, zeros_start, (src_blocks, block_mask, alpha_blocks))
    predicted = predicted.reshape(members, traces, S)
    partial_value = partial_value.transpose(1, 2, 0, 3).reshape(members, traces, S)
    return predicted, partial_value, block_terms


def normalize(vector):
    return vector / (jnp.sum(vector, axis=1, keepdims=True) / S)


def reference(src_emb, dst_emb, out_emb, word_table, log_norm, block_mask, tokens, alpha_start, beta_end):
    traces = tokens.shape[1]
    word_rows = word_table[tokens.reshape(-1)]
    logits = jnp.dot(word_rows, out_emb.T, preferred_element_type=jnp.float32)
    emission = jnp.exp(logits - log_norm[None, :]).reshape(STEPS, traces, S)
    alphas = [alpha_start]
    beta_store = {STEPS: beta_end}

    def weight_at(k):
        return (emission[k - 1] * beta_store[k]).astype(jnp.bfloat16)

    for k in range(1, STEPS):
        predicted, partial_value, _ = sweep(src_emb, dst_emb, block_mask, alphas[k - 1][None], weight_at(STEPS - k + 1)[None])
        alphas.append(normalize(predicted[0] * emission[k - 1]))
        beta_store[STEPS - k] = normalize(partial_value[0])
    final_alphas = jnp.stack(alphas)
    final_weights = jnp.stack([weight_at(t + 1) for t in range(STEPS)])
    predicted, partial_value, block_terms = sweep(src_emb, dst_emb, block_mask, final_alphas, final_weights)
    alpha_end = normalize(predicted[STEPS - 1] * emission[STEPS - 1])
    beta_start = normalize(partial_value[0])
    pair_total = jnp.sum(block_terms, axis=(0, 3))
    counts = jnp.sum(block_terms / pair_total[None, :, :, None], axis=(1, 2)) * (NB * NB / (STEPS * traces))
    return alpha_end, beta_start, counts
```

```python
import functools

import jax
import jax.numpy as jnp
from jax import lax
from jax.experimental import pallas as pl
from jax.experimental.pallas import tpu as pltpu
from jax.sharding import PartitionSpec as P

BLK = 512
CH = 256
STEPS = 3
TRACES = 8
TB = STEPS * TRACES
UNROLL = 4
very_negative = -1e30
VMEM_LIMIT = 52 * 1024 * 1024
NT = (((1,), (1,)), ((), ()))
NN = (((1,), (0,)), ((), ()))
f32 = jnp.float32
bf16 = jnp.bfloat16

OUT_AT = CH
WORD_AT = 2 * CH
BETA_AT = WORD_AT + 32
MISC_AT = BETA_AT + 48
BLOCK_ROWS = MISC_AT + 16


def tiles(x):
    return jnp.concatenate([x[:, :128], x[:, 128:]], axis=0)


def untile(x):
    return jnp.concatenate([x[:8], x[8:16]], axis=1)


def lanes(shape=(8, 128)):
    return lax.broadcasted_iota(jnp.int32, shape, len(shape) - 1)


def put_lanes(pairs):
    lane = lanes()
    out = jnp.zeros((8, 128), f32)
    for at, value in pairs:
        out = jnp.where(lane == at, value, out)
    return out


def inverse(x):
    return jnp.where(x > 0, 1.0 / jnp.where(x > 0, x, 1.0), 0.0)


def split3(x):
    hi = x.astype(bf16).astype(f32)
    rest = x - hi
    mid = rest.astype(bf16).astype(f32)
    return hi, mid, rest - mid


def place_of(p, A, H):
    return (p % A) * H + p // A


def pack_kernel(A, H, tok, words, dst, out, norm, beta, mask, block):
    vocab = words.shape[0]
    place = lax.axis_index("dst")
    ids = tok[...] - place * vocab
    onehot = jnp.where(lanes((TB, vocab)) == ids, 1.0, 0.0).astype(bf16)
    looked = lax.dot_general(onehot, words[...], NN, preferred_element_type=f32)
    looked = jnp.concatenate([looked, jnp.zeros((8, 128), f32)], axis=0).astype(bf16)
    RB = mask.shape[0]
    diag = lax.broadcasted_iota(jnp.int32, (RB, 128), 0) == lanes((RB, 128))
    for l in range(A):
        block[l, 0:CH] = dst[l * CH : (l + 1) * CH]
        block[l, OUT_AT : OUT_AT + CH] = out[l * CH : (l + 1) * CH]
        block[l, WORD_AT : WORD_AT + 32] = looked
        parts = split3(tiles(beta[:, l * CH : (l + 1) * CH]))
        block[l, BETA_AT : BETA_AT + 48] = jnp.concatenate(parts, axis=0).astype(bf16)
        column = mask[:, l // 2 : l // 2 + 1].astype(f32)
        mask_row = jnp.sum(jnp.where(diag, column, 0.0), axis=0, keepdims=True)
        norms = split3(norm[2 * l : 2 * l + 2])
        block[l, MISC_AT : MISC_AT + 16] = jnp.concatenate(
            [*norms, mask_row, jnp.zeros((9, 128), f32)], axis=0
        ).astype(bf16)


def table_kernel(
    A, H, recv, src, table, tops, best, pay, units, count,
    slots, mass, mask_v, mask_s, word_v, sems, mask_sem,
):
    RB = src.shape[0] // BLK
    for k in range(A):
        misc = recv[k, MISC_AT : MISC_AT + 16].astype(f32)
        mask_v[k : k + 1] = misc[6:7].astype(jnp.int32)
    copy = pltpu.make_async_copy(mask_v, mask_s, mask_sem)
    copy.start()
    best[...] = jnp.full(best.shape, very_negative, f32)
    mass[...] = jnp.zeros(mass.shape, f32)
    total = recv[0, WORD_AT : WORD_AT + 32].astype(f32)
    for k in range(1, A):
        total = total + recv[k, WORD_AT : WORD_AT + 32].astype(f32)
    word_v[...] = total
    copy.wait()

    def listing(i, c):
        for k in range(A):
            units[c] = i * A + k
            c = c + mask_s[k, i]
        return c

    cnt = lax.fori_loop(0, RB, listing, 0)
    count[0] = cnt

    def one(n, carry):
        u = units[n]
        i = u // A
        k = u - i * A
        cols = recv[k, 0:CH]
        for half in range(2):
            rows = src[pl.ds(i * BLK + half * CH, CH)]
            scores = lax.dot_general(cols, rows, NT, preferred_element_type=f32)
            top = jnp.max(scores, axis=0, keepdims=True)
            e = jnp.exp(scores - top)
            s = jnp.sum(e, axis=0, keepdims=True)
            at = slice(half * CH, (half + 1) * CH)
            slots[n, :, at] = e.astype(bf16)
            tops[i, pl.ds(k, 1), at] = top
            old = best[pl.ds(i, 1), at]
            new = jnp.maximum(old, top)
            mass[pl.ds(i, 1), at] = mass[pl.ds(i, 1), at] * jnp.exp(old - new) + s * jnp.exp(top - new)
            best[pl.ds(i, 1), at] = new
        pltpu.make_async_copy(slots.at[n], table.at[n], sems.at[n]).start()
        return carry

    lax.fori_loop(0, cnt, one, 0)
    per = TB // A
    mine = lax.axis_index("dst") // H
    words = word_v[pl.ds(mine * per, per)]
    for p in range(2 * RB):
        d = place_of(p, A, H)
        at = (p % 2) * CH
        i = p // 2
        pay[d, 0:1] = best[i : i + 1, at : at + 128]
        pay[d, 1:2] = best[i : i + 1, at + 128 : at + 256]
        pay[d, 2:3] = mass[i : i + 1, at : at + 128]
        pay[d, 3:4] = mass[i : i + 1, at + 128 : at + 256]
        pay[d, 4 : 4 + per] = words
        if pay.shape[1] > 4 + per:
            pay[d, 4 + per :] = jnp.zeros((pay.shape[1] - 4 - per, 128), f32)

    def drain(n, carry):
        pltpu.make_async_copy(slots.at[n], table.at[n], sems.at[n]).wait()
        return carry

    lax.fori_loop(0, cnt, drain, 0)


def start_table(table, slots, sems, cnt):
    def go(n, carry):
        pltpu.make_async_copy(table.at[n], slots.at[n], sems.at[n]).start()
        return carry

    lax.fori_loop(0, cnt, go, 0)


def sweep(A, table, slots, sems, units, cnt, unit_work):
    def some(it, carry):
        base = it * UNROLL
        for q in range(UNROLL):
            @pl.when(base + q < cnt)
            def _():
                n = base + q
                pltpu.make_async_copy(table.at[n], slots.at[n], sems.at[n]).wait()

        results = []
        for q in range(UNROLL):
            n = jnp.minimum(base + q, cnt - 1)
            u = units[n]
            i = u // A
            k = u - i * A
            results.append((i, k, base + q < cnt, unit_work(slots[n], i, k)))
        for i, k, valid, (adds) in results:
            for ref, index, value in adds:
                ref[index] += jnp.where(valid, value, 0.0)
        return carry

    lax.fori_loop(0, (cnt + UNROLL - 1) // UNROLL, some, 0)


def backward_unit(weights, factor, acc):
    def work(t, i, k):
        spread = lax.dot_general(weights[k], t, NN, preferred_element_type=f32)
        return [(acc, i, spread * factor(i, k))]

    return work


def scatter_rows(pay, acc, A, H, at=0):
    for p in range(2 * acc.shape[0]):
        part = acc[p // 2, :, (p % 2) * CH : (p % 2 + 1) * CH]
        pay[place_of(p, A, H), at : at + 16] = tiles(part)


def first_back_kernel(
    A, H, got, recv, tops, best, units, count, table,
    pay, share, emx, em_last, w_last, slots, acc, word_v, sems,
):
    cnt = count[0]
    start_table(table, slots, sems, cnt)
    D = A * H
    per = TB // A
    for l in range(A):
        total = got[l * H, 4 : 4 + per]
        for h in range(1, H):
            total = total + got[l * H + h, 4 : 4 + per]
        word_v[l * per : (l + 1) * per] = total
    words = word_v[0:TB].astype(bf16)
    top = got[0, 0:2]
    for d in range(1, D):
        top = jnp.maximum(top, got[d, 0:2])
    mass = jnp.zeros_like(top)
    for d in range(D):
        mass = mass + got[d, 2:4] * jnp.exp(got[d, 0:2] - top)
    log_total = top + jnp.log(mass)
    for d in range(D):
        share[d] = jnp.exp(got[d, 0:2] - log_total)
    mine = lax.axis_index("src")
    for k in range(A):
        logits = lax.dot_general(
            words, recv[k, OUT_AT : OUT_AT + CH], NT, preferred_element_type=f32
        )
        misc = recv[k, MISC_AT : MISC_AT + 16].astype(f32)
        norm = misc[0:2] + misc[2:4] + misc[4:6]
        norm = jnp.concatenate([norm[0:1], norm[1:2]], axis=1)
        em = jnp.exp(logits - norm)
        parts = recv[k, BETA_AT : BETA_AT + 48].astype(f32)
        beta = untile(parts[0:16] + parts[16:32] + parts[32:48])
        em_last[k] = em[16:24]
        w_last[k] = (em[16:24] * beta).astype(bf16)

        @pl.when(mine == k)
        def _():
            emx[...] = em

    acc[...] = jnp.zeros(acc.shape, f32)

    def factor(i, k):
        return jnp.exp(tops[i, pl.ds(k, 1)] - best[pl.ds(i, 1)])

    sweep(A, table, slots, sems, units, cnt, backward_unit(w_last, factor, acc))
    scatter_rows(pay, acc, A, H)
    tail = jnp.concatenate([log_total, jnp.zeros((6, 128), f32)], axis=0)
    for d in range(D):
        pay[d, 16:24] = tail


def send_weights(pay, carried, emission, A):
    whole = jnp.sum(carried[0:8] + carried[8:16], axis=1, keepdims=True)
    scaled = tiles(emission * (untile(carried) * inverse(whole)))
    for k in range(A):
        pay[k, 16:32] = scaled
    return whole


def first_forward_kernel(
    A, H, got, share, alpha, tops, emx, units, count, table,
    pay, factor, slots, acc, sems,
):
    cnt = count[0]
    start_table(table, slots, sems, cnt)
    D = A * H
    RB = tops.shape[0]
    for i in range(RB):
        d0 = place_of(2 * i, A, H)
        d1 = place_of(2 * i + 1, A, H)
        log_total = jnp.concatenate(
            [got[d0, 16:17], got[d0, 17:18], got[d1, 16:17], got[d1, 17:18]], axis=1
        )
        factor[i] = jnp.exp(tops[i] - log_total)
    acc[...] = jnp.zeros(acc.shape, f32)

    def work(t, i, k):
        mix = alpha[:, pl.ds(pl.multiple_of(i * BLK, BLK), BLK)] * factor[i, pl.ds(k, 1)]
        pred = lax.dot_general(mix.astype(bf16), t, NT, preferred_element_type=f32)
        return [(acc, k, pred)]

    sweep(A, table, slots, sems, units, cnt, work)
    for k in range(A):
        pay[k, 0:16] = tiles(acc[k])
    first = jnp.zeros((8, 128), f32)
    second = jnp.zeros((8, 128), f32)
    for d in range(D):
        first = first + got[d, 0:8] * share[d, 0:1]
        second = second + got[d, 8:16] * share[d, 1:2]
    whole = send_weights(pay, jnp.concatenate([first, second], axis=0), emx[8:16], A)
    for k in range(A):
        pay[k, 32:40] = put_lanes([(0, whole)])


def forward_kernel(
    A, H, t_at, last, got, factor, w_other, em, held, units, count, table, *rest
):
    if last:
        em_last, terms_in, pay, terms, carried_out, scales, slots, acc, alpha, sems = rest
    else:
        pay, terms, scales, slots, acc, alpha, sems = rest
    cnt = count[0]
    start_table(table, slots, sems, cnt)
    D = A * H
    RB = factor.shape[0]
    total = got[0, 16:24] + got[0, 24:32]
    for d in range(1, D):
        total = total + (got[d, 16:24] + got[d, 24:32])
    rows_sum = jnp.sum(total, axis=1, keepdims=True)
    scale = inverse(rows_sum)
    for p in range(2 * RB):
        u = got[place_of(p, A, H), 16:32]
        alpha[p // 2, :, (p % 2) * CH : (p % 2 + 1) * CH] = untile(u) * scale
    acc[...] = jnp.zeros(acc.shape, f32)
    terms[...] = terms_in[...] if last else jnp.zeros(terms.shape, f32)
    lane = lanes()

    def work(t, i, k):
        mix = alpha[i] * factor[i, pl.ds(k, 1)]
        pred = lax.dot_general(mix.astype(bf16), t, NT, preferred_element_type=f32)
        term = jnp.sum(pred * w_other[k].astype(f32), axis=1, keepdims=True)
        return [(acc, k, pred), (terms, k, jnp.where(lane == t_at * RB + i, term, 0.0))]

    sweep(A, table, slots, sems, units, cnt, work)
    for k in range(A):
        pay[k, 0:16] = tiles(acc[k])
    cols_sum = got[0, 32:40]
    for d in range(1, D):
        cols_sum = cols_sum + got[d, 32:40]
    norm = inverse(cols_sum)
    first = jnp.zeros((8, 128), f32)
    second = jnp.zeros((8, 128), f32)
    for d in range(D):
        weight = got[d, 32:40] * norm
        first = first + got[d, 0:8] * weight
        second = second + got[d, 8:16] * weight
    carried = jnp.concatenate([first, second], axis=0)
    sigma = (held[...] * norm)[:, 0:1]
    if not last:
        whole = send_weights(pay, carried, em[0:8], A)
        for k in range(A):
            pay[k, 32:40] = put_lanes([(0, whole), (1, rows_sum)])
        scales[...] = put_lanes([(0, sigma), (1, rows_sum)])
        return
    carried_out[...] = carried
    reach = jnp.zeros((8, 128), f32)
    every = jnp.zeros((8, 128), f32)
    for k in range(A):
        product = acc[k] * em_last[k]
        reach = reach + (product[:, :128] + product[:, 128:])
        every = every + terms[k]
    reach = jnp.sum(reach, axis=1, keepdims=True)
    whole = jnp.sum(first + second, axis=1, keepdims=True)
    ratio_one = em[:, 0:1]
    pairs = []
    for t in range(STEPS):
        here = (lane >= t * RB) & (lane < (t + 1) * RB)
        pairs.append(jnp.sum(jnp.where(here, every, 0.0), axis=1, keepdims=True))
    tail = put_lanes(
        [(0, rows_sum), (1, reach), (2, whole), (3, pairs[0] * sigma), (4, pairs[1] * ratio_one), (5, pairs[2])]
    )
    for k in range(A):
        pay[k, 16:24] = tail
    scales[...] = put_lanes([(0, sigma), (1, ratio_one), (2, rows_sum)])


def back_kernel(
    A, H, states, t_at, got, factor, emx, units, count, table, *rest
):
    if t_at is None:
        pay, weights, held, slots, acc, sems = rest
    else:
        alpha, terms_in, scales_in, pay, terms, ratio, held, slots, acc, weights, sems = rest
    cnt = count[0]
    start_table(table, slots, sems, cnt)
    D = A * H
    RB = factor.shape[0]
    cols_sum = got[0, 32:40, 0:1]
    for k in range(1, A):
        cols_sum = cols_sum + got[k, 32:40, 0:1]
    norm = inverse(cols_sum)
    for k in range(A):
        weights[k] = (untile(got[k, 16:32]) * (got[k, 32:40, 0:1] * norm)).astype(bf16)
    acc[...] = jnp.zeros(acc.shape, f32)
    if t_at is None:
        work = backward_unit(weights, lambda i, k: factor[i, pl.ds(k, 1)], acc)
    else:
        terms[...] = terms_in[...]
        lane = lanes()

        def work(t, i, k):
            spread = lax.dot_general(weights[k], t, NN, preferred_element_type=f32)
            fac = factor[i, pl.ds(k, 1)]
            mix = (alpha[:, pl.ds(pl.multiple_of(i * BLK, BLK), BLK)] * fac).astype(bf16)
            term = jnp.sum(mix.astype(f32) * spread, axis=1, keepdims=True)
            return [
                (acc, i, spread * fac),
                (terms, k, jnp.where(lane == t_at * RB + i, term, 0.0)),
            ]

    sweep(A, table, slots, sems, units, cnt, work)
    scatter_rows(pay, acc, A, H)
    if t_at is None:
        pred = got[0, 0:16]
        for s in range(1, A):
            pred = pred + got[s, 0:16]
        emission = emx[0:8]
    else:
        rows_sum = got[0, 32:40, 1:2]
        for s in range(1, A):
            rows_sum = rows_sum + got[s, 32:40, 1:2]
        inv = inverse(rows_sum)
        pred = jnp.zeros((16, 128), f32)
        for s in range(A):
            weight = got[s, 32:40, 1:2] * inv * states
            pred = pred + got[s, 0:16] * jnp.concatenate([weight, weight], axis=0)
        emission = emx[8:16]
        rho = scales_in[:, 1:2] * inv
        ratio[...] = put_lanes([(0, rho * scales_in[:, 0:1])])
    product = tiles(untile(pred) * emission)
    wide = jnp.broadcast_to(cols_sum, (8, 128))
    held[...] = wide
    for d in range(D):
        pay[d, 16:32] = product
        pay[d, 32:40] = wide


def gather_kernel(A, H, states, RB, got, carried, emx, terms, scales, pay):
    rows_sum = got[0, 16:24, 0:1]
    for s in range(1, A):
        rows_sum = rows_sum + got[s, 16:24, 0:1]
    inv = inverse(rows_sum)
    pred = jnp.zeros((16, 128), f32)
    tail = jnp.zeros((8, 128), f32)
    lane = lanes()
    for s in range(A):
        share = got[s, 16:24, 0:1] * inv
        weight = share * states
        pred = pred + got[s, 0:16] * jnp.concatenate([weight, weight], axis=0)
        piece = got[s, 16:24]
        piece = jnp.where(lane == 1, piece * weight, piece)
        piece = jnp.where(lane == 5, piece * share, piece)
        tail = tail + piece
    product = tiles(untile(pred) * emx[16:24])
    tail = jnp.where(lane < 6, tail, 0.0)
    tail = jnp.concatenate([tail[:, 64:], tail[:, :64]], axis=1)
    sigma = scales[:, 0:1]
    one = scales[:, 1:2]
    rho = scales[:, 2:3] * inv
    mult = jnp.where(lane < RB, sigma, jnp.where(lane < 2 * RB, one, jnp.where(lane < 3 * RB, rho, 0.0)))
    for k in range(A):
        last = jnp.where(lane < 3 * RB, terms[k] * mult, 0.0) + tail
        for h in range(H):
            pay[k * H + h, 32:40] = last
    back = carried[...]
    for d in range(A * H):
        pay[d, 0:16] = back
        pay[d, 16:32] = product


def finish_kernel(A, H, states, scale, RB, got, alpha, beta, counts):
    D = A * H
    lane = lanes()
    total = got[0, 32:40]
    for d in range(1, D):
        total = total + got[d, 32:40]
    total = jnp.where(lane >= 64, total, 0.0)
    reach = total[:, 65:66]
    whole = total[:, 66:67]
    for_beta = states / whole
    for_alpha = states / reach
    inv = jnp.zeros((8, 128), f32)
    for t in range(STEPS):
        here = (lane >= t * RB) & (lane < (t + 1) * RB)
        inv = jnp.where(here, scale / total[:, 67 + t : 68 + t], inv)
    for p in range(2 * RB):
        beta[:, p * CH : (p + 1) * CH] = untile(got[place_of(p, A, H), 0:16]) * for_beta
    mine = lax.rem(lax.axis_index("dst"), H)
    row = lax.broadcasted_iota(jnp.int32, (RB, 128), 0)
    wide = lanes((RB, 128))
    picks = (wide == row) | (wide == row + RB) | (wide == row + 2 * RB)
    out = jnp.zeros((RB, 128), f32)
    for l in range(A):
        alpha[:, l * CH : (l + 1) * CH] = untile(got[l * H + mine, 16:32]) * for_alpha
        line = jnp.where(lane < 3 * RB, got[l * H + mine, 32:40] * inv, 0.0)
        line = jnp.sum(line, axis=0, keepdims=True)
        column = jnp.sum(jnp.where(picks, line, 0.0), axis=1, keepdims=True)
        out = out + jnp.where(wide == l // 2, column, 0.0)
    counts[...] = out[:, : counts.shape[1]]


def call(body, outs, scratch=(), big=False):
    vm = pl.BlockSpec(memory_space=pltpu.VMEM)
    sm = pl.BlockSpec(memory_space=pltpu.SMEM)
    hbm = pl.BlockSpec(memory_space=pl.ANY)
    kinds = {"v": vm, "s": sm, "h": hbm}

    def run(kinds_in, *args):
        return pl.pallas_call(
            body,
            in_specs=[kinds[c] for c in kinds_in],
            out_specs=[kinds[c] for c, _, _ in outs],
            out_shape=[jax.ShapeDtypeStruct(s, d) for _, s, d in outs],
            scratch_shapes=list(scratch),
            compiler_params=pltpu.CompilerParams(
                vmem_limit_bytes=VMEM_LIMIT if big else 16 * 1024 * 1024
            ),
        )(*args)

    return run


def local(
    src_emb, dst_emb, out_emb, word_table, log_norm, block_mask, tokens, alpha_start, beta_end
):
    A = lax.axis_size("src")
    D = lax.axis_size("dst")
    H = D // A
    rows = src_emb.shape[0]
    RB = rows // BLK
    states = float(rows * A)
    NB = RB * A
    UN = RB * A
    VM = pltpu.VMEM
    groups = [[h + H * k for k in range(A)] for h in range(H)]
    over_dst = lambda x: lax.all_to_all(x, "dst", 0, 0)
    over_src = lambda x: lax.all_to_all(x, "src", 0, 0)
    part = functools.partial

    (block,) = call(part(pack_kernel, A, H), [("v", (A, BLOCK_ROWS, 128), bf16)], big=True)(
        "vvvvvvv", tokens.reshape(TB, 1), word_table, dst_emb, out_emb,
        log_norm.reshape(-1, 128), beta_end, block_mask,
    )
    recv = lax.all_to_all(block, "dst", 0, 0, axis_index_groups=groups)

    per = TB // A
    pay_rows = -(-(4 + per) // 8) * 8
    slots = VM((UN, CH, BLK), bf16)
    sems = pltpu.SemaphoreType.DMA((UN,))
    acc_rows = VM((RB, 8, BLK), f32)
    acc_cols = VM((A, 8, CH), f32)
    table, tops, best, pay, units, count = call(
        part(table_kernel, A, H),
        [
            ("h", (UN, CH, BLK), bf16),
            ("v", (RB, A, BLK), f32),
            ("v", (RB, BLK), f32),
            ("v", (D, pay_rows, 128), f32),
            ("s", (UN,), jnp.int32),
            ("s", (1,), jnp.int32),
        ],
        [
            slots, VM((RB, BLK), f32), VM((A, 128), jnp.int32),
            pltpu.SMEM((A, 128), jnp.int32), VM((32, 128), f32), sems, pltpu.SemaphoreType.DMA(()),
        ],
        big=True,
    )("vv", recv, src_emb)
    got = over_dst(pay)

    pay, share, emx, em_last, w_last = call(
        part(first_back_kernel, A, H),
        [
            ("v", (D, 24, 128), f32),
            ("v", (D, 2, 128), f32),
            ("v", (TB, CH), f32),
            ("v", (A, 8, CH), f32),
            ("v", (A, 8, CH), bf16),
        ],
        [slots, acc_rows, VM((TB, 128), f32), sems],
        big=True,
    )("vvvvssh", got, recv, tops, best, units, count, table)
    got = over_dst(pay)

    pay, factor = call(
        part(first_forward_kernel, A, H),
        [("v", (A, 40, 128), f32), ("v", (RB, A, BLK), f32)],
        [slots, acc_cols, sems],
        big=True,
    )("vvvvvssh", got, share, alpha_start, tops, emx, units, count, table)
    got = over_src(pay)

    pay, w_two, held = call(
        part(back_kernel, A, H, states, None),
        [("v", (D, 40, 128), f32), ("v", (A, 8, CH), bf16), ("v", (8, 128), f32)],
        [slots, acc_rows, sems],
        big=True,
    )("vvvssh", got, factor, emx, units, count, table)
    got = over_dst(pay)

    pay, terms, scales = call(
        part(forward_kernel, A, H, 1, False),
        [("v", (A, 40, 128), f32), ("v", (A, 8, 128), f32), ("v", (8, 128), f32)],
        [slots, acc_cols, acc_rows, sems],
        big=True,
    )("vvvvvssh", got, factor, w_two, emx, held, units, count, table)
    got = over_src(pay)

    pay, terms, ratio, held = call(
        part(back_kernel, A, H, states, 0),
        [
            ("v", (D, 40, 128), f32), ("v", (A, 8, 128), f32),
            ("v", (8, 128), f32), ("v", (8, 128), f32),
        ],
        [slots, acc_rows, VM((A, 8, CH), bf16), sems],
        big=True,
    )("vvvsshvvv", got, factor, emx, units, count, table, alpha_start, terms, scales)
    got = over_dst(pay)

    pay, terms, carried, scales = call(
        part(forward_kernel, A, H, 2, True),
        [
            ("v", (A, 24, 128), f32), ("v", (A, 8, 128), f32),
            ("v", (16, 128), f32), ("v", (8, 128), f32),
        ],
        [slots, acc_cols, acc_rows, sems],
        big=True,
    )("vvvvvsshvv", got, factor, w_last, ratio, held, units, count, table, em_last, terms)
    got = over_src(pay)

    (pay,) = call(part(gather_kernel, A, H, states, RB), [("v", (D, 40, 128), f32)])(
        "vvvvv", got, carried, emx, terms, scales
    )
    got = over_dst(pay)

    alpha_end, beta_start, counts = call(
        part(finish_kernel, A, H, states, NB * NB / TB, RB),
        [
            ("v", (8, A * CH), f32),
            ("v", (8, rows), f32),
            ("v", (RB, block_mask.shape[1]), f32),
        ],
    )("v", got)
    swaps = [
        (a * D + b * H + h, b * D + a * H + h) for a in range(A) for b in range(A) for h in range(H)
    ]
    alpha_end = lax.ppermute(alpha_end, ("src", "dst"), swaps)
    return (alpha_end, beta_start, counts)


def solution(mesh):
    return jax.shard_map(
        local,
        mesh=mesh,
        in_specs=(
            P("src", None),
            P("dst", None),
            P("dst", None),
            P("dst", None),
            P("dst"),
            P("src", "dst"),
            P(),
            P(None, "src"),
            P(None, "dst"),
        ),
        out_specs=(P(None, "dst"), P(None, "src"), P("src", "dst")),
        check_vma=False,
    )
```

```python
import functools

import jax
import jax.numpy as jnp
from jax import lax
from jax.experimental import pallas as pl
from jax.experimental.pallas import tpu as pltpu
from jax.sharding import PartitionSpec as P

BLK = 512
CH = 256
STEPS = 3
TRACES = 8
TB = STEPS * TRACES
UNROLL = 4
very_negative = -1e30
VMEM_LIMIT = int(20.5 * 1024 * 1024)
NT = (((1,), (1,)), ((), ()))
NN = (((1,), (0,)), ((), ()))
f32 = jnp.float32
bf16 = jnp.bfloat16

OUT_AT = CH
WORD_AT = 2 * CH
BETA_AT = WORD_AT + 32
MISC_AT = BETA_AT + 48
BLOCK_ROWS = MISC_AT + 16


def tiles(x):
    return jnp.concatenate([x[:, :128], x[:, 128:]], axis=0)


def untile(x):
    return jnp.concatenate([x[:8], x[8:16]], axis=1)


def lanes(shape=(8, 128)):
    return lax.broadcasted_iota(jnp.int32, shape, len(shape) - 1)


def put_lanes(pairs):
    lane = lanes()
    out = jnp.zeros((8, 128), f32)
    for at, value in pairs:
        out = jnp.where(lane == at, value, out)
    return out


def inverse(x):
    return jnp.where(x > 0, 1.0 / jnp.where(x > 0, x, 1.0), 0.0)


def split3(x):
    hi = x.astype(bf16).astype(f32)
    rest = x - hi
    mid = rest.astype(bf16).astype(f32)
    return hi, mid, rest - mid


def place_of(p, A, H):
    return (p % A) * H + p // A


def pack_kernel(A, H, tok, words, dst, out, norm, beta, mask, block):
    vocab = words.shape[0]
    place = lax.axis_index("dst")
    ids = tok[...] - place * vocab
    onehot = jnp.where(lanes((TB, vocab)) == ids, 1.0, 0.0).astype(bf16)
    looked = lax.dot_general(onehot, words[...], NN, preferred_element_type=f32)
    looked = jnp.concatenate([looked, jnp.zeros((8, 128), f32)], axis=0).astype(bf16)
    RB = mask.shape[0]
    diag = lax.broadcasted_iota(jnp.int32, (RB, 128), 0) == lanes((RB, 128))
    for l in range(A):
        block[l, 0:CH] = dst[l * CH : (l + 1) * CH]
        block[l, OUT_AT : OUT_AT + CH] = out[l * CH : (l + 1) * CH]
        block[l, WORD_AT : WORD_AT + 32] = looked
        parts = split3(tiles(beta[:, l * CH : (l + 1) * CH]))
        block[l, BETA_AT : BETA_AT + 48] = jnp.concatenate(parts, axis=0).astype(bf16)
        column = mask[:, l // 2 : l // 2 + 1].astype(f32)
        mask_row = jnp.sum(jnp.where(diag, column, 0.0), axis=0, keepdims=True)
        norms = split3(norm[2 * l : 2 * l + 2])
        block[l, MISC_AT : MISC_AT + 16] = jnp.concatenate(
            [*norms, mask_row, jnp.zeros((9, 128), f32)], axis=0
        ).astype(bf16)


def table_kernel(
    A, H, recv, src, table, tops, best, pay, units, count,
    mass, mask_v, mask_s, word_v, mask_sem,
):
    RB = src.shape[0] // BLK
    for k in range(A):
        misc = recv[k, MISC_AT : MISC_AT + 16].astype(f32)
        mask_v[k : k + 1] = misc[6:7].astype(jnp.int32)
    copy = pltpu.make_async_copy(mask_v, mask_s, mask_sem)
    copy.start()
    best[...] = jnp.full(best.shape, very_negative, f32)
    mass[...] = jnp.zeros(mass.shape, f32)
    total = recv[0, WORD_AT : WORD_AT + 32].astype(f32)
    for k in range(1, A):
        total = total + recv[k, WORD_AT : WORD_AT + 32].astype(f32)
    word_v[...] = total
    copy.wait()

    def listing(i, c):
        for k in range(A):
            units[c] = i * A + k
            c = c + mask_s[k, i]
        return c

    cnt = lax.fori_loop(0, RB, listing, 0)
    count[0] = cnt

    def one(n, carry):
        u = units[n]
        i = u // A
        k = u - i * A
        cols = recv[k, 0:CH]
        for half in range(2):
            rows = src[pl.ds(i * BLK + half * CH, CH)]
            scores = lax.dot_general(cols, rows, NT, preferred_element_type=f32)
            top = jnp.max(scores, axis=0, keepdims=True)
            e = jnp.exp(scores - top)
            s = jnp.sum(e, axis=0, keepdims=True)
            at = slice(half * CH, (half + 1) * CH)
            table[n, :, at] = e.astype(bf16)
            tops[i, pl.ds(k, 1), at] = top
            old = best[pl.ds(i, 1), at]
            new = jnp.maximum(old, top)
            mass[pl.ds(i, 1), at] = mass[pl.ds(i, 1), at] * jnp.exp(old - new) + s * jnp.exp(top - new)
            best[pl.ds(i, 1), at] = new
        return carry

    lax.fori_loop(0, cnt, one, 0)
    per = TB // A
    mine = lax.axis_index("dst") // H
    words = word_v[pl.ds(mine * per, per)]
    for p in range(2 * RB):
        d = place_of(p, A, H)
        at = (p % 2) * CH
        i = p // 2
        pay[d, 0:1] = best[i : i + 1, at : at + 128]
        pay[d, 1:2] = best[i : i + 1, at + 128 : at + 256]
        pay[d, 2:3] = mass[i : i + 1, at : at + 128]
        pay[d, 3:4] = mass[i : i + 1, at + 128 : at + 256]
        pay[d, 4 : 4 + per] = words
        if pay.shape[1] > 4 + per:
            pay[d, 4 + per :] = jnp.zeros((pay.shape[1] - 4 - per, 128), f32)


def sweep(A, table, units, cnt, unit_work):
    def some(it, carry):
        base = it * UNROLL
        results = []
        for q in range(UNROLL):
            n = jnp.minimum(base + q, cnt - 1)
            u = units[n]
            i = u // A
            k = u - i * A
            results.append((i, k, base + q < cnt, unit_work(table[n], i, k)))
        for i, k, valid, (adds) in results:
            for ref, index, value in adds:
                ref[index] += jnp.where(valid, value, 0.0)
        return carry

    lax.fori_loop(0, (cnt + UNROLL - 1) // UNROLL, some, 0)


def backward_unit(weights, factor, acc):
    def work(t, i, k):
        spread = lax.dot_general(weights[k], t, NN, preferred_element_type=f32)
        return [(acc, i, spread * factor(i, k))]

    return work


def scatter_rows(pay, acc, A, H, at=0):
    for p in range(2 * acc.shape[0]):
        part = acc[p // 2, :, (p % 2) * CH : (p % 2 + 1) * CH]
        pay[place_of(p, A, H), at : at + 16] = tiles(part)


def first_back_kernel(
    A, H, got, recv, tops, best, units, count, table,
    pay, share, emx, em_last, w_last, acc, word_v,
):
    cnt = count[0]
    D = A * H
    per = TB // A
    for l in range(A):
        total = got[l * H, 4 : 4 + per]
        for h in range(1, H):
            total = total + got[l * H + h, 4 : 4 + per]
        word_v[l * per : (l + 1) * per] = total
    words = word_v[0:TB].astype(bf16)
    top = got[0, 0:2]
    for d in range(1, D):
        top = jnp.maximum(top, got[d, 0:2])
    mass = jnp.zeros_like(top)
    for d in range(D):
        mass = mass + got[d, 2:4] * jnp.exp(got[d, 0:2] - top)
    log_total = top + jnp.log(mass)
    for d in range(D):
        share[d] = jnp.exp(got[d, 0:2] - log_total)
    mine = lax.axis_index("src")
    for k in range(A):
        logits = lax.dot_general(
            words, recv[k, OUT_AT : OUT_AT + CH], NT, preferred_element_type=f32
        )
        misc = recv[k, MISC_AT : MISC_AT + 16].astype(f32)
        norm = misc[0:2] + misc[2:4] + misc[4:6]
        norm = jnp.concatenate([norm[0:1], norm[1:2]], axis=1)
        em = jnp.exp(logits - norm)
        parts = recv[k, BETA_AT : BETA_AT + 48].astype(f32)
        beta = untile(parts[0:16] + parts[16:32] + parts[32:48])
        em_last[k] = em[16:24]
        w_last[k] = (em[16:24] * beta).astype(bf16)

        @pl.when(mine == k)
        def _():
            emx[...] = em

    acc[...] = jnp.zeros(acc.shape, f32)

    def factor(i, k):
        return jnp.exp(tops[i, pl.ds(k, 1)] - best[pl.ds(i, 1)])

    sweep(A, table, units, cnt, backward_unit(w_last, factor, acc))
    scatter_rows(pay, acc, A, H)
    tail = jnp.concatenate([log_total, jnp.zeros((6, 128), f32)], axis=0)
    for d in range(D):
        pay[d, 16:24] = tail


def send_weights(pay, carried, emission, A):
    whole = jnp.sum(carried[0:8] + carried[8:16], axis=1, keepdims=True)
    scaled = tiles(emission * (untile(carried) * inverse(whole)))
    for k in range(A):
        pay[k, 16:32] = scaled
    return whole


def first_forward_kernel(
    A, H, got, share, alpha, tops, emx, units, count, table,
    pay, factor, acc,
):
    cnt = count[0]
    D = A * H
    RB = tops.shape[0]
    for i in range(RB):
        d0 = place_of(2 * i, A, H)
        d1 = place_of(2 * i + 1, A, H)
        log_total = jnp.concatenate(
            [got[d0, 16:17], got[d0, 17:18], got[d1, 16:17], got[d1, 17:18]], axis=1
        )
        factor[i] = jnp.exp(tops[i] - log_total)
    acc[...] = jnp.zeros(acc.shape, f32)

    def work(t, i, k):
        mix = alpha[:, pl.ds(pl.multiple_of(i * BLK, BLK), BLK)] * factor[i, pl.ds(k, 1)]
        pred = lax.dot_general(mix.astype(bf16), t, NT, preferred_element_type=f32)
        return [(acc, k, pred)]

    sweep(A, table, units, cnt, work)
    for k in range(A):
        pay[k, 0:16] = tiles(acc[k])
    first = jnp.zeros((8, 128), f32)
    second = jnp.zeros((8, 128), f32)
    for d in range(D):
        first = first + got[d, 0:8] * share[d, 0:1]
        second = second + got[d, 8:16] * share[d, 1:2]
    whole = send_weights(pay, jnp.concatenate([first, second], axis=0), emx[8:16], A)
    for k in range(A):
        pay[k, 32:40] = put_lanes([(0, whole)])


def forward_kernel(
    A, H, t_at, last, got, factor, w_other, em, held, units, count, table, *rest
):
    if last:
        em_last, terms_in, pay, terms, carried_out, scales, acc, alpha = rest
    else:
        pay, terms, scales, acc, alpha = rest
    cnt = count[0]
    D = A * H
    RB = factor.shape[0]
    total = got[0, 16:24] + got[0, 24:32]
    for d in range(1, D):
        total = total + (got[d, 16:24] + got[d, 24:32])
    rows_sum = jnp.sum(total, axis=1, keepdims=True)
    scale = inverse(rows_sum)
    for p in range(2 * RB):
        u = got[place_of(p, A, H), 16:32]
        alpha[p // 2, :, (p % 2) * CH : (p % 2 + 1) * CH] = untile(u) * scale
    acc[...] = jnp.zeros(acc.shape, f32)
    terms[...] = terms_in[...] if last else jnp.zeros(terms.shape, f32)
    lane = lanes()

    def work(t, i, k):
        mix = alpha[i] * factor[i, pl.ds(k, 1)]
        pred = lax.dot_general(mix.astype(bf16), t, NT, preferred_element_type=f32)
        term = jnp.sum(pred * w_other[k].astype(f32), axis=1, keepdims=True)
        return [(acc, k, pred), (terms, k, jnp.where(lane == t_at * RB + i, term, 0.0))]

    sweep(A, table, units, cnt, work)
    for k in range(A):
        pay[k, 0:16] = tiles(acc[k])
    cols_sum = got[0, 32:40]
    for d in range(1, D):
        cols_sum = cols_sum + got[d, 32:40]
    norm = inverse(cols_sum)
    first = jnp.zeros((8, 128), f32)
    second = jnp.zeros((8, 128), f32)
    for d in range(D):
        weight = got[d, 32:40] * norm
        first = first + got[d, 0:8] * weight
        second = second + got[d, 8:16] * weight
    carried = jnp.concatenate([first, second], axis=0)
    sigma = (held[...] * norm)[:, 0:1]
    if not last:
        whole = send_weights(pay, carried, em[0:8], A)
        for k in range(A):
            pay[k, 32:40] = put_lanes([(0, whole), (1, rows_sum)])
        scales[...] = put_lanes([(0, sigma), (1, rows_sum)])
        return
    carried_out[...] = carried
    reach = jnp.zeros((8, 128), f32)
    every = jnp.zeros((8, 128), f32)
    for k in range(A):
        product = acc[k] * em_last[k]
        reach = reach + (product[:, :128] + product[:, 128:])
        every = every + terms[k]
    reach = jnp.sum(reach, axis=1, keepdims=True)
    whole = jnp.sum(first + second, axis=1, keepdims=True)
    ratio_one = em[:, 0:1]
    pairs = []
    for t in range(STEPS):
        here = (lane >= t * RB) & (lane < (t + 1) * RB)
        pairs.append(jnp.sum(jnp.where(here, every, 0.0), axis=1, keepdims=True))
    tail = put_lanes(
        [(0, rows_sum), (1, reach), (2, whole), (3, pairs[0] * sigma), (4, pairs[1] * ratio_one), (5, pairs[2])]
    )
    for k in range(A):
        pay[k, 16:24] = tail
    scales[...] = put_lanes([(0, sigma), (1, ratio_one), (2, rows_sum)])


def back_kernel(
    A, H, states, t_at, got, factor, emx, units, count, table, *rest
):
    if t_at is None:
        pay, weights, held, acc = rest
    else:
        alpha, terms_in, scales_in, pay, terms, ratio, held, acc, weights = rest
    cnt = count[0]
    D = A * H
    RB = factor.shape[0]
    cols_sum = got[0, 32:40, 0:1]
    for k in range(1, A):
        cols_sum = cols_sum + got[k, 32:40, 0:1]
    norm = inverse(cols_sum)
    for k in range(A):
        weights[k] = (untile(got[k, 16:32]) * (got[k, 32:40, 0:1] * norm)).astype(bf16)
    acc[...] = jnp.zeros(acc.shape, f32)
    if t_at is None:
        work = backward_unit(weights, lambda i, k: factor[i, pl.ds(k, 1)], acc)
    else:
        terms[...] = terms_in[...]
        lane = lanes()

        def work(t, i, k):
            spread = lax.dot_general(weights[k], t, NN, preferred_element_type=f32)
            fac = factor[i, pl.ds(k, 1)]
            mix = (alpha[:, pl.ds(pl.multiple_of(i * BLK, BLK), BLK)] * fac).astype(bf16)
            term = jnp.sum(mix.astype(f32) * spread, axis=1, keepdims=True)
            return [
                (acc, i, spread * fac),
                (terms, k, jnp.where(lane == t_at * RB + i, term, 0.0)),
            ]

    sweep(A, table, units, cnt, work)
    scatter_rows(pay, acc, A, H)
    if t_at is None:
        pred = got[0, 0:16]
        for s in range(1, A):
            pred = pred + got[s, 0:16]
        emission = emx[0:8]
    else:
        rows_sum = got[0, 32:40, 1:2]
        for s in range(1, A):
            rows_sum = rows_sum + got[s, 32:40, 1:2]
        inv = inverse(rows_sum)
        pred = jnp.zeros((16, 128), f32)
        for s in range(A):
            weight = got[s, 32:40, 1:2] * inv * states
            pred = pred + got[s, 0:16] * jnp.concatenate([weight, weight], axis=0)
        emission = emx[8:16]
        rho = scales_in[:, 1:2] * inv
        ratio[...] = put_lanes([(0, rho * scales_in[:, 0:1])])
    product = tiles(untile(pred) * emission)
    wide = jnp.broadcast_to(cols_sum, (8, 128))
    held[...] = wide
    for d in range(D):
        pay[d, 16:32] = product
        pay[d, 32:40] = wide


def gather_kernel(A, H, states, RB, got, carried, emx, terms, scales, pay):
    rows_sum = got[0, 16:24, 0:1]
    for s in range(1, A):
        rows_sum = rows_sum + got[s, 16:24, 0:1]
    inv = inverse(rows_sum)
    pred = jnp.zeros((16, 128), f32)
    tail = jnp.zeros((8, 128), f32)
    lane = lanes()
    for s in range(A):
        share = got[s, 16:24, 0:1] * inv
        weight = share * states
        pred = pred + got[s, 0:16] * jnp.concatenate([weight, weight], axis=0)
        piece = got[s, 16:24]
        piece = jnp.where(lane == 1, piece * weight, piece)
        piece = jnp.where(lane == 5, piece * share, piece)
        tail = tail + piece
    product = tiles(untile(pred) * emx[16:24])
    tail = jnp.where(lane < 6, tail, 0.0)
    tail = jnp.concatenate([tail[:, 64:], tail[:, :64]], axis=1)
    sigma = scales[:, 0:1]
    one = scales[:, 1:2]
    rho = scales[:, 2:3] * inv
    mult = jnp.where(lane < RB, sigma, jnp.where(lane < 2 * RB, one, jnp.where(lane < 3 * RB, rho, 0.0)))
    for k in range(A):
        last = jnp.where(lane < 3 * RB, terms[k] * mult, 0.0) + tail
        for h in range(H):
            pay[k * H + h, 32:40] = last
    back = carried[...]
    for d in range(A * H):
        pay[d, 0:16] = back
        pay[d, 16:32] = product


def finish_kernel(A, H, states, scale, RB, got, alpha, beta, counts):
    D = A * H
    lane = lanes()
    total = got[0, 32:40]
    for d in range(1, D):
        total = total + got[d, 32:40]
    total = jnp.where(lane >= 64, total, 0.0)
    reach = total[:, 65:66]
    whole = total[:, 66:67]
    for_beta = states / whole
    for_alpha = states / reach
    inv = jnp.zeros((8, 128), f32)
    for t in range(STEPS):
        here = (lane >= t * RB) & (lane < (t + 1) * RB)
        inv = jnp.where(here, scale / total[:, 67 + t : 68 + t], inv)
    for p in range(2 * RB):
        beta[:, p * CH : (p + 1) * CH] = untile(got[place_of(p, A, H), 0:16]) * for_beta
    mine = lax.rem(lax.axis_index("dst"), H)
    row = lax.broadcasted_iota(jnp.int32, (RB, 128), 0)
    wide = lanes((RB, 128))
    picks = (wide == row) | (wide == row + RB) | (wide == row + 2 * RB)
    out = jnp.zeros((RB, 128), f32)
    for l in range(A):
        alpha[:, l * CH : (l + 1) * CH] = untile(got[l * H + mine, 16:32]) * for_alpha
        line = jnp.where(lane < 3 * RB, got[l * H + mine, 32:40] * inv, 0.0)
        line = jnp.sum(line, axis=0, keepdims=True)
        column = jnp.sum(jnp.where(picks, line, 0.0), axis=1, keepdims=True)
        out = out + jnp.where(wide == l // 2, column, 0.0)
    counts[...] = out[:, : counts.shape[1]]


def call(body, outs, scratch=(), big=False):
    vm = pl.BlockSpec(memory_space=pltpu.VMEM)
    sm = pl.BlockSpec(memory_space=pltpu.SMEM)
    hbm = pl.BlockSpec(memory_space=pl.ANY)
    kinds = {"v": vm, "s": sm, "h": hbm, "m": vm}

    def run(kinds_in, *args):
        return pl.pallas_call(
            body,
            in_specs=[kinds[c] for c in kinds_in],
            out_specs=[kinds[c] for c, _, _ in outs],
            out_shape=[
                pltpu.VMEM(s, d) if c == "m" else jax.ShapeDtypeStruct(s, d) for c, s, d in outs
            ],
            scratch_shapes=list(scratch),
            compiler_params=pltpu.CompilerParams(
                vmem_limit_bytes=VMEM_LIMIT if big else 16 * 1024 * 1024
            ),
        )(
            *[
                pltpu.with_memory_space_constraint(a, pltpu.VMEM) if c == "m" else a
                for c, a in zip(kinds_in, args)
            ]
        )

    return run


def local(
    src_emb, dst_emb, out_emb, word_table, log_norm, block_mask, tokens, alpha_start, beta_end
):
    A = lax.axis_size("src")
    D = lax.axis_size("dst")
    H = D // A
    rows = src_emb.shape[0]
    RB = rows // BLK
    states = float(rows * A)
    NB = RB * A
    UN = RB * A
    VM = pltpu.VMEM
    groups = [[h + H * k for k in range(A)] for h in range(H)]
    over_dst = lambda x: lax.all_to_all(x, "dst", 0, 0)
    over_src = lambda x: lax.all_to_all(x, "src", 0, 0)
    part = functools.partial

    (block,) = call(part(pack_kernel, A, H), [("v", (A, BLOCK_ROWS, 128), bf16)], big=True)(
        "vvvvvvv", tokens.reshape(TB, 1), word_table, dst_emb, out_emb,
        log_norm.reshape(-1, 128), beta_end, block_mask,
    )
    recv = lax.all_to_all(block, "dst", 0, 0, axis_index_groups=groups)

    per = TB // A
    pay_rows = -(-(4 + per) // 8) * 8
    acc_rows = VM((RB, 8, BLK), f32)
    acc_cols = VM((A, 8, CH), f32)
    table, tops, best, pay, units, count = call(
        part(table_kernel, A, H),
        [
            ("m", (UN, CH, BLK), bf16),
            ("v", (RB, A, BLK), f32),
            ("v", (RB, BLK), f32),
            ("v", (D, pay_rows, 128), f32),
            ("s", (UN,), jnp.int32),
            ("s", (1,), jnp.int32),
        ],
        [
            VM((RB, BLK), f32), VM((A, 128), jnp.int32),
            pltpu.SMEM((A, 128), jnp.int32), VM((32, 128), f32), pltpu.SemaphoreType.DMA(()),
        ],
        big=True,
    )("vv", recv, src_emb)
    got = over_dst(pay)

    pay, share, emx, em_last, w_last = call(
        part(first_back_kernel, A, H),
        [
            ("v", (D, 24, 128), f32),
            ("v", (D, 2, 128), f32),
            ("v", (TB, CH), f32),
            ("v", (A, 8, CH), f32),
            ("v", (A, 8, CH), bf16),
        ],
        [acc_rows, VM((TB, 128), f32)],
        big=True,
    )("vvvvssm", got, recv, tops, best, units, count, table)
    got = over_dst(pay)

    pay, factor = call(
        part(first_forward_kernel, A, H),
        [("v", (A, 40, 128), f32), ("v", (RB, A, BLK), f32)],
        [acc_cols],
        big=True,
    )("vvvvvssm", got, share, alpha_start, tops, emx, units, count, table)
    got = over_src(pay)

    pay, w_two, held = call(
        part(back_kernel, A, H, states, None),
        [("v", (D, 40, 128), f32), ("v", (A, 8, CH), bf16), ("v", (8, 128), f32)],
        [acc_rows],
        big=True,
    )("vvvssm", got, factor, emx, units, count, table)
    got = over_dst(pay)

    pay, terms, scales = call(
        part(forward_kernel, A, H, 1, False),
        [("v", (A, 40, 128), f32), ("v", (A, 8, 128), f32), ("v", (8, 128), f32)],
        [acc_cols, acc_rows],
        big=True,
    )("vvvvvssm", got, factor, w_two, emx, held, units, count, table)
    got = over_src(pay)

    pay, terms, ratio, held = call(
        part(back_kernel, A, H, states, 0),
        [
            ("v", (D, 40, 128), f32), ("v", (A, 8, 128), f32),
            ("v", (8, 128), f32), ("v", (8, 128), f32),
        ],
        [acc_rows, VM((A, 8, CH), bf16)],
        big=True,
    )("vvvssmvvv", got, factor, emx, units, count, table, alpha_start, terms, scales)
    got = over_dst(pay)

    pay, terms, carried, scales = call(
        part(forward_kernel, A, H, 2, True),
        [
            ("v", (A, 24, 128), f32), ("v", (A, 8, 128), f32),
            ("v", (16, 128), f32), ("v", (8, 128), f32),
        ],
        [acc_cols, acc_rows],
        big=True,
    )("vvvvvssmvv", got, factor, w_last, ratio, held, units, count, table, em_last, terms)
    got = over_src(pay)

    (pay,) = call(part(gather_kernel, A, H, states, RB), [("v", (D, 40, 128), f32)])(
        "vvvvv", got, carried, emx, terms, scales
    )
    got = over_dst(pay)

    alpha_end, beta_start, counts = call(
        part(finish_kernel, A, H, states, NB * NB / TB, RB),
        [
            ("v", (8, A * CH), f32),
            ("v", (8, rows), f32),
            ("v", (RB, block_mask.shape[1]), f32),
        ],
    )("v", got)
    swaps = [
        (a * D + b * H + h, b * D + a * H + h) for a in range(A) for b in range(A) for h in range(H)
    ]
    alpha_end = lax.ppermute(alpha_end, ("src", "dst"), swaps)
    return (alpha_end, beta_start, counts)


def solution(mesh):
    return jax.shard_map(
        local,
        mesh=mesh,
        in_specs=(
            P("src", None),
            P("dst", None),
            P("dst", None),
            P("dst", None),
            P("dst"),
            P("src", "dst"),
            P(),
            P(None, "src"),
            P(None, "dst"),
        ),
        out_specs=(P(None, "dst"), P(None, "src"), P("src", "dst")),
        check_vma=False,
    )
```

```python
import functools

import jax
import jax.numpy as jnp
from jax import lax
from jax.experimental import pallas as pl
from jax.experimental.pallas import tpu as pltpu
from jax.sharding import PartitionSpec as P

BLK = 512
CH = 256
STEPS = 3
TRACES = 8
TB = STEPS * TRACES
UNROLL = 8
TABLE_UNROLL = 4
very_negative = -1e30
VMEM_LIMIT = int(20.5 * 1024 * 1024)
NT = (((1,), (1,)), ((), ()))
NN = (((1,), (0,)), ((), ()))
f32 = jnp.float32
bf16 = jnp.bfloat16

OUT_AT = CH
WORD_AT = 2 * CH
BETA_AT = WORD_AT + 32
MISC_AT = BETA_AT + 48
BLOCK_ROWS = MISC_AT + 16


def tiles(x):
    return jnp.concatenate([x[:, :128], x[:, 128:]], axis=0)


def untile(x):
    return jnp.concatenate([x[:8], x[8:16]], axis=1)


def lanes(shape=(8, 128)):
    return lax.broadcasted_iota(jnp.int32, shape, len(shape) - 1)


def put_lanes(pairs):
    lane = lanes()
    out = jnp.zeros((8, 128), f32)
    for at, value in pairs:
        out = jnp.where(lane == at, value, out)
    return out


def inverse(x):
    return jnp.where(x > 0, 1.0 / jnp.where(x > 0, x, 1.0), 0.0)


def split3(x):
    hi = x.astype(bf16).astype(f32)
    rest = x - hi
    mid = rest.astype(bf16).astype(f32)
    return hi, mid, rest - mid


def place_of(p, A, H):
    return (p % A) * H + p // A


def pack_kernel(
    A, H, tok, words, dst, out, norm, beta, mask,
    block, words_v, norm_v, beta_v, mask_v, tok_s, sems,
):
    copies = [
        pltpu.make_async_copy(words, words_v, sems.at[0]),
        pltpu.make_async_copy(norm, norm_v, sems.at[1]),
        pltpu.make_async_copy(beta, beta_v, sems.at[2]),
        pltpu.make_async_copy(mask, mask_v, sems.at[3]),
    ]
    for l in range(A):
        rows = slice(l * CH, (l + 1) * CH)
        copies.append(pltpu.make_async_copy(dst.at[rows], block.at[l, 0:CH], sems.at[4 + 2 * l]))
        copies.append(
            pltpu.make_async_copy(out.at[rows], block.at[l, OUT_AT : OUT_AT + CH], sems.at[5 + 2 * l])
        )
    tok_copy = pltpu.make_async_copy(tok, tok_s, sems.at[4 + 2 * A])
    tok_copy.start()
    for copy in copies:
        copy.start()
    tok_copy.wait()
    vocab = words.shape[0]
    place = lax.axis_index("dst")
    row = lax.broadcasted_iota(jnp.int32, (TB, 1), 0)
    ids = jnp.zeros((TB, 1), jnp.int32)
    for r in range(TB):
        ids = jnp.where(row == r, tok_s[r // TRACES, r % TRACES], ids)
    onehot = jnp.where(lanes((TB, vocab)) == ids - place * vocab, 1.0, 0.0).astype(bf16)
    for copy in copies[:4]:
        copy.wait()
    looked = lax.dot_general(onehot, words_v[...], NN, preferred_element_type=f32)
    looked = jnp.concatenate([looked, jnp.zeros((8, 128), f32)], axis=0).astype(bf16)
    width, RB = mask_v.shape
    for l in range(A):
        block[l, WORD_AT : WORD_AT + 32] = looked
        parts = split3(tiles(beta_v[:, l * CH : (l + 1) * CH]))
        block[l, BETA_AT : BETA_AT + 48] = jnp.concatenate(parts, axis=0).astype(bf16)
        mask_row = mask_v[l // 2 : l // 2 + 1].astype(f32)
        mask_row = jnp.concatenate([mask_row, jnp.zeros((1, 128 - RB), f32)], axis=1)
        norms = split3(norm_v[2 * l : 2 * l + 2])
        block[l, MISC_AT : MISC_AT + 16] = jnp.concatenate(
            [*norms, mask_row, jnp.zeros((9, 128), f32)], axis=0
        ).astype(bf16)
    for copy in copies[4:]:
        copy.wait()


def table_kernel(
    A, H, recv, src, table, tops, best, pay, units, count,
    sums, mass, mask_v, mask_s, word_v, mask_sem,
):
    RB = src.shape[0] // BLK
    for k in range(A):
        misc = recv[k, MISC_AT : MISC_AT + 16].astype(f32)
        mask_v[k : k + 1] = misc[6:7].astype(jnp.int32)
    copy = pltpu.make_async_copy(mask_v, mask_s, mask_sem)
    copy.start()
    tops[...] = jnp.full(tops.shape, very_negative, f32)
    sums[...] = jnp.zeros(sums.shape, f32)
    total = recv[0, WORD_AT : WORD_AT + 32].astype(f32)
    for k in range(1, A):
        total = total + recv[k, WORD_AT : WORD_AT + 32].astype(f32)
    word_v[...] = total
    copy.wait()

    def listing(i, c):
        for k in range(A):
            units[c] = i * A + k
            c = c + mask_s[k, i]
        return c

    cnt = lax.fori_loop(0, RB, listing, 0)
    count[0] = cnt

    def some(it, carry):
        for q in range(TABLE_UNROLL):
            n = jnp.minimum(it * TABLE_UNROLL + q, cnt - 1)
            u = units[n]
            i = u // A
            k = u - i * A
            cols = recv[k, 0:CH]
            unit_tops, unit_sums = [], []
            for part in range(BLK // 128):
                rows = src[pl.ds(pl.multiple_of(i * BLK + part * 128, 128), 128)]
                scores = lax.dot_general(cols, rows, NT, preferred_element_type=f32)
                top = jnp.max(scores, axis=0, keepdims=True)
                e = jnp.exp(scores - top)
                unit_tops.append(top)
                unit_sums.append(jnp.sum(e, axis=0, keepdims=True))
                table[n, :, part * 128 : (part + 1) * 128] = e.astype(bf16)
            tops[i, pl.ds(k, 1)] = jnp.concatenate(unit_tops, axis=1)
            sums[i, pl.ds(k, 1)] = jnp.concatenate(unit_sums, axis=1)
        return carry

    lax.fori_loop(0, (cnt + TABLE_UNROLL - 1) // TABLE_UNROLL, some, 0)
    for i in range(RB):
        row_best = jnp.max(tops[i], axis=0, keepdims=True)
        best[i : i + 1] = row_best
        mass[i : i + 1] = jnp.sum(sums[i] * jnp.exp(tops[i] - row_best), axis=0, keepdims=True)
    per = TB // A
    mine = lax.axis_index("dst") // H
    words = word_v[pl.ds(mine * per, per)]
    for p in range(2 * RB):
        d = place_of(p, A, H)
        at = (p % 2) * CH
        i = p // 2
        pay[d, 0:1] = best[i : i + 1, at : at + 128]
        pay[d, 1:2] = best[i : i + 1, at + 128 : at + 256]
        pay[d, 2:3] = mass[i : i + 1, at : at + 128]
        pay[d, 3:4] = mass[i : i + 1, at + 128 : at + 256]
        pay[d, 4 : 4 + per] = words
        if pay.shape[1] > 4 + per:
            pay[d, 4 + per :] = jnp.zeros((pay.shape[1] - 4 - per, 128), f32)


def sweep(A, table, units, cnt, unit_work):
    def some(it, carry):
        base = it * UNROLL
        results = []
        for q in range(UNROLL):
            n = jnp.minimum(base + q, cnt - 1)
            u = units[n]
            i = u // A
            k = u - i * A
            results.append((i, k, base + q < cnt, unit_work(table[n], i, k)))
        for i, k, valid, (adds) in results:
            for ref, index, value in adds:
                ref[index] += jnp.where(valid, value, 0.0)
        return carry

    lax.fori_loop(0, (cnt + UNROLL - 1) // UNROLL, some, 0)


def backward_unit(weights, factor, acc):
    def work(t, i, k):
        spread = lax.dot_general(weights[k], t, NN, preferred_element_type=f32)
        return [(acc, i, spread * factor(i, k))]

    return work


def halves(x):
    hi = x.astype(bf16)
    return hi, (x - hi.astype(f32)).astype(bf16)


def scatter_rows(pay, acc, A, H, exact=False):
    for p in range(2 * acc.shape[0]):
        part = tiles(acc[p // 2, :, (p % 2) * CH : (p % 2 + 1) * CH])
        d = place_of(p, A, H)
        if exact:
            hi, lo = halves(part)
            pay[d, 0:16] = hi
            pay[d, 16:32] = lo
        else:
            pay[d, 0:16] = part.astype(bf16)


def first_back_kernel(
    A, H, got, recv, tops, best, units, count, table,
    pay, share, emx, em_last, w_last, acc, word_v,
):
    cnt = count[0]
    D = A * H
    per = TB // A
    for l in range(A):
        total = got[l * H, 4 : 4 + per]
        for h in range(1, H):
            total = total + got[l * H + h, 4 : 4 + per]
        word_v[l * per : (l + 1) * per] = total
    words = word_v[0:TB].astype(bf16)
    top = got[0, 0:2]
    for d in range(1, D):
        top = jnp.maximum(top, got[d, 0:2])
    mass = jnp.zeros_like(top)
    for d in range(D):
        mass = mass + got[d, 2:4] * jnp.exp(got[d, 0:2] - top)
    log_total = top + jnp.log(mass)
    for d in range(D):
        share[d] = jnp.exp(got[d, 0:2] - log_total)
    mine = lax.axis_index("src")
    for k in range(A):
        logits = lax.dot_general(
            words, recv[k, OUT_AT : OUT_AT + CH], NT, preferred_element_type=f32
        )
        misc = recv[k, MISC_AT : MISC_AT + 16].astype(f32)
        norm = misc[0:2] + misc[2:4] + misc[4:6]
        norm = jnp.concatenate([norm[0:1], norm[1:2]], axis=1)
        em = jnp.exp(logits - norm)
        parts = recv[k, BETA_AT : BETA_AT + 48].astype(f32)
        beta = untile(parts[0:16] + parts[16:32] + parts[32:48])
        em_last[k] = em[16:24]
        w_last[k] = (em[16:24] * beta).astype(bf16)

        @pl.when(mine == k)
        def _():
            emx[...] = em

    acc[...] = jnp.zeros(acc.shape, f32)

    def factor(i, k):
        return jnp.exp(tops[i, pl.ds(k, 1)] - best[pl.ds(i, 1)])

    sweep(A, table, units, cnt, backward_unit(w_last, factor, acc))
    scatter_rows(pay, acc, A, H)
    tail = jnp.concatenate([*split3(log_total), jnp.zeros((10, 128), f32)], axis=0).astype(bf16)
    for d in range(D):
        pay[d, 16:32] = tail


def send_weights(pay, carried, emission, A):
    whole = jnp.sum(carried[0:8] + carried[8:16], axis=1, keepdims=True)
    scaled = tiles(emission * (untile(carried) * inverse(whole)))
    for k in range(A):
        pay[k, 16:32] = scaled
    return whole


def first_forward_kernel(
    A, H, got, share, alpha, tops, emx, units, count, table,
    pay, factor, acc,
):
    cnt = count[0]
    D = A * H
    RB = tops.shape[0]
    for i in range(RB):
        pieces = []
        for p in (2 * i, 2 * i + 1):
            total = got[place_of(p, A, H), 16:32].astype(f32)
            total = total[0:2] + total[2:4] + total[4:6]
            pieces += [total[0:1], total[1:2]]
        log_total = jnp.concatenate(pieces, axis=1)
        factor[i] = jnp.exp(tops[i] - log_total)
    acc[...] = jnp.zeros(acc.shape, f32)

    def work(t, i, k):
        mix = alpha[:, pl.ds(pl.multiple_of(i * BLK, BLK), BLK)] * factor[i, pl.ds(k, 1)]
        pred = lax.dot_general(mix.astype(bf16), t, NT, preferred_element_type=f32)
        return [(acc, k, pred)]

    sweep(A, table, units, cnt, work)
    for k in range(A):
        pay[k, 0:16] = tiles(acc[k])
    first = jnp.zeros((8, 128), f32)
    second = jnp.zeros((8, 128), f32)
    for d in range(D):
        piece = got[d, 0:16].astype(f32)
        first = first + piece[0:8] * share[d, 0:1]
        second = second + piece[8:16] * share[d, 1:2]
    whole = send_weights(pay, jnp.concatenate([first, second], axis=0), emx[8:16], A)
    for k in range(A):
        pay[k, 32:40] = put_lanes([(0, whole)])


def forward_kernel(
    A, H, t_at, last, got, factor, w_other, em, held, units, count, table, *rest
):
    if last:
        em_last, terms_in, pay, terms, carried_out, scales, acc, alpha = rest
    else:
        pay, terms, scales, acc, alpha = rest
    cnt = count[0]
    D = A * H
    RB = factor.shape[0]
    at = 32 if last else 16
    total = got[0, at : at + 16].astype(f32)
    for d in range(1, D):
        total = total + got[d, at : at + 16].astype(f32)
    total = total[0:8] + total[8:16]
    rows_sum = jnp.sum(total, axis=1, keepdims=True)
    scale = inverse(rows_sum)
    for p in range(2 * RB):
        u = got[place_of(p, A, H), at : at + 16].astype(f32)
        alpha[p // 2, :, (p % 2) * CH : (p % 2 + 1) * CH] = untile(u) * scale
    acc[...] = jnp.zeros(acc.shape, f32)
    terms[...] = terms_in[...] if last else jnp.zeros(terms.shape, f32)
    lane = lanes()

    def work(t, i, k):
        mix = alpha[i] * factor[i, pl.ds(k, 1)]
        pred = lax.dot_general(mix.astype(bf16), t, NT, preferred_element_type=f32)
        term = jnp.sum(pred * w_other[k].astype(f32), axis=1, keepdims=True)
        return [(acc, k, pred), (terms, k, jnp.where(lane == t_at * RB + i, term, 0.0))]

    sweep(A, table, units, cnt, work)
    for k in range(A):
        pay[k, 0:16] = tiles(acc[k])
    spans = [got[d, at + 16 : at + 32].astype(f32) for d in range(D)]
    spans = [x[0:8] + x[8:16] for x in spans]
    cols_sum = spans[0]
    for d in range(1, D):
        cols_sum = cols_sum + spans[d]
    norm = inverse(cols_sum)
    first = jnp.zeros((8, 128), f32)
    second = jnp.zeros((8, 128), f32)
    for d in range(D):
        weight = spans[d] * norm
        piece = got[d, 0:16].astype(f32)
        if last:
            piece = piece + got[d, 16:32].astype(f32)
        first = first + piece[0:8] * weight
        second = second + piece[8:16] * weight
    carried = jnp.concatenate([first, second], axis=0)
    sigma = (held[...] * norm)[:, 0:1]
    if not last:
        whole = send_weights(pay, carried, em[0:8], A)
        for k in range(A):
            pay[k, 32:40] = put_lanes([(0, whole), (1, rows_sum)])
        scales[...] = put_lanes([(0, sigma), (1, rows_sum)])
        return
    carried_out[...] = carried
    reach = jnp.zeros((8, 128), f32)
    every = jnp.zeros((8, 128), f32)
    for k in range(A):
        product = acc[k] * em_last[k]
        reach = reach + (product[:, :128] + product[:, 128:])
        every = every + terms[k]
    reach = jnp.sum(reach, axis=1, keepdims=True)
    whole = jnp.sum(first + second, axis=1, keepdims=True)
    ratio_one = em[:, 0:1]
    pairs = []
    for t in range(STEPS):
        here = (lane >= t * RB) & (lane < (t + 1) * RB)
        pairs.append(jnp.sum(jnp.where(here, every, 0.0), axis=1, keepdims=True))
    tail = put_lanes(
        [(0, rows_sum), (1, reach), (2, whole), (3, pairs[0] * sigma), (4, pairs[1] * ratio_one), (5, pairs[2])]
    )
    for k in range(A):
        pay[k, 16:24] = tail
    scales[...] = put_lanes([(0, sigma), (1, ratio_one), (2, rows_sum)])


def back_kernel(
    A, H, states, t_at, got, factor, emx, units, count, table, *rest
):
    if t_at is None:
        pay, weights, held, acc = rest
    else:
        alpha, terms_in, scales_in, pay, terms, ratio, held, acc, weights = rest
    cnt = count[0]
    D = A * H
    RB = factor.shape[0]
    cols_sum = got[0, 32:40, 0:1]
    for k in range(1, A):
        cols_sum = cols_sum + got[k, 32:40, 0:1]
    norm = inverse(cols_sum)
    for k in range(A):
        weights[k] = (untile(got[k, 16:32]) * (got[k, 32:40, 0:1] * norm)).astype(bf16)
    acc[...] = jnp.zeros(acc.shape, f32)
    if t_at is None:
        work = backward_unit(weights, lambda i, k: factor[i, pl.ds(k, 1)], acc)
    else:
        terms[...] = terms_in[...]
        lane = lanes()

        def work(t, i, k):
            spread = lax.dot_general(weights[k], t, NN, preferred_element_type=f32)
            fac = factor[i, pl.ds(k, 1)]
            mix = (alpha[:, pl.ds(pl.multiple_of(i * BLK, BLK), BLK)] * fac).astype(bf16)
            term = jnp.sum(mix.astype(f32) * spread, axis=1, keepdims=True)
            return [
                (acc, i, spread * fac),
                (terms, k, jnp.where(lane == t_at * RB + i, term, 0.0)),
            ]

    sweep(A, table, units, cnt, work)
    scatter_rows(pay, acc, A, H, exact=t_at is not None)
    if t_at is None:
        pred = got[0, 0:16]
        for s in range(1, A):
            pred = pred + got[s, 0:16]
        emission = emx[0:8]
    else:
        rows_sum = got[0, 32:40, 1:2]
        for s in range(1, A):
            rows_sum = rows_sum + got[s, 32:40, 1:2]
        inv = inverse(rows_sum)
        pred = jnp.zeros((16, 128), f32)
        for s in range(A):
            weight = got[s, 32:40, 1:2] * inv * states
            pred = pred + got[s, 0:16] * jnp.concatenate([weight, weight], axis=0)
        emission = emx[8:16]
        rho = scales_in[:, 1:2] * inv
        ratio[...] = put_lanes([(0, rho * scales_in[:, 0:1])])
    product = tiles(untile(pred) * emission).astype(bf16)
    wide = jnp.broadcast_to(cols_sum, (8, 128))
    held[...] = wide
    wide = jnp.concatenate(halves(wide), axis=0)
    at = 16 if t_at is None else 32
    for d in range(D):
        pay[d, at : at + 16] = product
        pay[d, at + 16 : at + 32] = wide


def gather_kernel(A, H, states, RB, got, carried, emx, terms, scales, pay):
    rows_sum = got[0, 16:24, 0:1]
    for s in range(1, A):
        rows_sum = rows_sum + got[s, 16:24, 0:1]
    inv = inverse(rows_sum)
    pred = jnp.zeros((16, 128), f32)
    tail = jnp.zeros((8, 128), f32)
    lane = lanes()
    for s in range(A):
        share = got[s, 16:24, 0:1] * inv
        weight = share * states
        pred = pred + got[s, 0:16] * jnp.concatenate([weight, weight], axis=0)
        piece = got[s, 16:24]
        piece = jnp.where(lane == 1, piece * weight, piece)
        piece = jnp.where(lane == 5, piece * share, piece)
        tail = tail + piece
    product = tiles(untile(pred) * emx[16:24])
    tail = jnp.where(lane < 6, tail, 0.0)
    tail = jnp.concatenate([tail[:, 64:], tail[:, :64]], axis=1)
    sigma = scales[:, 0:1]
    one = scales[:, 1:2]
    rho = scales[:, 2:3] * inv
    mult = jnp.where(lane < RB, sigma, jnp.where(lane < 2 * RB, one, jnp.where(lane < 3 * RB, rho, 0.0)))
    for k in range(A):
        last = jnp.where(lane < 3 * RB, terms[k] * mult, 0.0) + tail
        for h in range(H):
            pay[k * H + h, 32:40] = last
    back = carried[...]
    for d in range(A * H):
        pay[d, 0:16] = back
        pay[d, 16:32] = product


def finish_kernel(A, H, states, scale, RB, got, alpha, beta, counts):
    D = A * H
    lane = lanes()
    total = got[0, 32:40]
    for d in range(1, D):
        total = total + got[d, 32:40]
    total = jnp.where(lane >= 64, total, 0.0)
    reach = total[:, 65:66]
    whole = total[:, 66:67]
    for_beta = states / whole
    for_alpha = states / reach
    inv = jnp.zeros((8, 128), f32)
    for t in range(STEPS):
        here = (lane >= t * RB) & (lane < (t + 1) * RB)
        inv = jnp.where(here, scale / total[:, 67 + t : 68 + t], inv)
    for p in range(2 * RB):
        beta[:, p * CH : (p + 1) * CH] = untile(got[place_of(p, A, H), 0:16]) * for_beta
    mine = lax.rem(lax.axis_index("dst"), H)
    row = lax.broadcasted_iota(jnp.int32, (RB, 128), 0)
    wide = lanes((RB, 128))
    picks = (wide == row) | (wide == row + RB) | (wide == row + 2 * RB)
    out = jnp.zeros((RB, 128), f32)
    for l in range(A):
        alpha[:, l * CH : (l + 1) * CH] = untile(got[l * H + mine, 16:32]) * for_alpha
        line = jnp.where(lane < 3 * RB, got[l * H + mine, 32:40] * inv, 0.0)
        line = jnp.sum(line, axis=0, keepdims=True)
        column = jnp.sum(jnp.where(picks, line, 0.0), axis=1, keepdims=True)
        out = out + jnp.where(wide == l // 2, column, 0.0)
    counts[...] = out[:, : counts.shape[1]]


def call(body, outs, scratch=(), big=False):
    vm = pl.BlockSpec(memory_space=pltpu.VMEM)
    sm = pl.BlockSpec(memory_space=pltpu.SMEM)
    hbm = pl.BlockSpec(memory_space=pl.ANY)
    kinds = {"v": vm, "s": sm, "h": hbm, "m": vm}
    spaces = {"m": pltpu.VMEM, "h": pltpu.HBM}

    def run(kinds_in, *args):
        return pl.pallas_call(
            body,
            in_specs=[kinds[c] for c in kinds_in],
            out_specs=[kinds[c] for c, _, _ in outs],
            out_shape=[
                spaces[c](s, d) if c in spaces else jax.ShapeDtypeStruct(s, d) for c, s, d in outs
            ],
            scratch_shapes=list(scratch),
            compiler_params=pltpu.CompilerParams(
                vmem_limit_bytes=VMEM_LIMIT if big else 16 * 1024 * 1024
            ),
        )(
            *[
                pltpu.with_memory_space_constraint(a, spaces[c]) if c in spaces else a
                for c, a in zip(kinds_in, args)
            ]
        )

    return run


def local(
    src_emb, dst_emb, out_emb, word_table, log_norm, block_mask, tokens, alpha_start, beta_end
):
    A = lax.axis_size("src")
    D = lax.axis_size("dst")
    H = D // A
    rows = src_emb.shape[0]
    RB = rows // BLK
    states = float(rows * A)
    NB = RB * A
    UN = RB * A
    VM = pltpu.VMEM
    groups = [[h + H * k for k in range(A)] for h in range(H)]
    over_dst = lambda x: lax.all_to_all(x, "dst", 0, 0)
    over_src = lambda x: lax.all_to_all(x, "src", 0, 0)
    part = functools.partial

    (block,) = call(
        part(pack_kernel, A, H),
        [("v", (A, BLOCK_ROWS, 128), bf16)],
        [
            VM(word_table.shape, bf16), VM((dst_emb.shape[0] // 128, 128), f32),
            VM(beta_end.shape, f32), VM(block_mask.shape[::-1], jnp.int32),
            pltpu.SMEM(tokens.shape, jnp.int32), pltpu.SemaphoreType.DMA((5 + 2 * A,)),
        ],
    )(
        "hhhhhhh", tokens, word_table, dst_emb, out_emb,
        log_norm.reshape(-1, 128), beta_end, block_mask.T,
    )
    recv = lax.all_to_all(block, "dst", 0, 0, axis_index_groups=groups)

    per = TB // A
    pay_rows = -(-(4 + per) // 8) * 8
    acc_rows = VM((RB, 8, BLK), f32)
    acc_cols = VM((A, 8, CH), f32)
    table, tops, best, pay, units, count = call(
        part(table_kernel, A, H),
        [
            ("m", (UN, CH, BLK), bf16),
            ("v", (RB, A, BLK), f32),
            ("v", (RB, BLK), f32),
            ("v", (D, pay_rows, 128), f32),
            ("s", (UN,), jnp.int32),
            ("s", (1,), jnp.int32),
        ],
        [
            VM((RB, A, BLK), f32), VM((RB, BLK), f32), VM((A, 128), jnp.int32),
            pltpu.SMEM((A, 128), jnp.int32), VM((32, 128), f32), pltpu.SemaphoreType.DMA(()),
        ],
        big=True,
    )("vv", recv, src_emb)
    got = over_dst(pay)

    pay, share, emx, em_last, w_last = call(
        part(first_back_kernel, A, H),
        [
            ("v", (D, 32, 128), bf16),
            ("v", (D, 2, 128), f32),
            ("v", (TB, CH), f32),
            ("v", (A, 8, CH), f32),
            ("v", (A, 8, CH), bf16),
        ],
        [acc_rows, VM((TB, 128), f32)],
        big=True,
    )("vvvvssm", got, recv, tops, best, units, count, table)
    got = over_dst(pay)

    pay, factor = call(
        part(first_forward_kernel, A, H),
        [("v", (A, 40, 128), f32), ("v", (RB, A, BLK), f32)],
        [acc_cols],
        big=True,
    )("vvvvvssm", got, share, alpha_start, tops, emx, units, count, table)
    got = over_src(pay)

    pay, w_two, held = call(
        part(back_kernel, A, H, states, None),
        [("v", (D, 48, 128), bf16), ("v", (A, 8, CH), bf16), ("v", (8, 128), f32)],
        [acc_rows],
        big=True,
    )("vvvssm", got, factor, emx, units, count, table)
    got = over_dst(pay)

    pay, terms, scales = call(
        part(forward_kernel, A, H, 1, False),
        [("v", (A, 40, 128), f32), ("v", (A, 8, 128), f32), ("v", (8, 128), f32)],
        [acc_cols, acc_rows],
        big=True,
    )("vvvvvssm", got, factor, w_two, emx, held, units, count, table)
    got = over_src(pay)

    pay, terms, ratio, held = call(
        part(back_kernel, A, H, states, 0),
        [
            ("v", (D, 64, 128), bf16), ("v", (A, 8, 128), f32),
            ("v", (8, 128), f32), ("v", (8, 128), f32),
        ],
        [acc_rows, VM((A, 8, CH), bf16)],
        big=True,
    )("vvvssmvvv", got, factor, emx, units, count, table, alpha_start, terms, scales)
    got = over_dst(pay)

    pay, terms, carried, scales = call(
        part(forward_kernel, A, H, 2, True),
        [
            ("v", (A, 24, 128), f32), ("v", (A, 8, 128), f32),
            ("v", (16, 128), f32), ("v", (8, 128), f32),
        ],
        [acc_cols, acc_rows],
        big=True,
    )("vvvvvssmvv", got, factor, w_last, ratio, held, units, count, table, em_last, terms)
    got = over_src(pay)

    (pay,) = call(part(gather_kernel, A, H, states, RB), [("v", (D, 40, 128), f32)])(
        "vvvvv", got, carried, emx, terms, scales
    )
    got = over_dst(pay)

    alpha_end, beta_start, counts = call(
        part(finish_kernel, A, H, states, NB * NB / TB, RB),
        [
            ("v", (8, A * CH), f32),
            ("v", (8, rows), f32),
            ("v", (RB, block_mask.shape[1]), f32),
        ],
    )("v", got)
    swaps = [
        (a * D + b * H + h, b * D + a * H + h) for a in range(A) for b in range(A) for h in range(H)
    ]
    alpha_end = lax.ppermute(alpha_end, ("src", "dst"), swaps)
    return (alpha_end, beta_start, counts)


def solution(mesh):
    return jax.shard_map(
        local,
        mesh=mesh,
        in_specs=(
            P("src", None),
            P("dst", None),
            P("dst", None),
            P("dst", None),
            P("dst"),
            P("src", "dst"),
            P(),
            P(None, "src"),
            P(None, "dst"),
        ),
        out_specs=(P(None, "dst"), P(None, "src"), P("src", "dst")),
        check_vma=False,
    )
```

```python
import functools

import jax
import jax.numpy as jnp
from jax import lax
from jax.experimental import pallas as pl
from jax.experimental.pallas import tpu as pltpu
from jax.sharding import PartitionSpec as P

BLK = 512
CH = 256
STEPS = 3
TRACES = 8
TB = STEPS * TRACES
UNROLL = 8
LARGE = 24
TABLE_UNROLL = 4
very_negative = -1e30
VMEM_LIMIT = int(20.5 * 1024 * 1024)
NT = (((1,), (1,)), ((), ()))
NN = (((1,), (0,)), ((), ()))
f32 = jnp.float32
bf16 = jnp.bfloat16

OUT_AT = CH
WORD_AT = 2 * CH
BETA_AT = WORD_AT + 32
MISC_AT = BETA_AT + 48
BLOCK_ROWS = MISC_AT + 16


def tiles(x):
    return jnp.concatenate([x[:, :128], x[:, 128:]], axis=0)


def untile(x):
    return jnp.concatenate([x[:8], x[8:16]], axis=1)


def lanes(shape=(8, 128)):
    return lax.broadcasted_iota(jnp.int32, shape, len(shape) - 1)


def put_lanes(pairs):
    lane = lanes()
    out = jnp.zeros((8, 128), f32)
    for at, value in pairs:
        out = jnp.where(lane == at, value, out)
    return out


def place_lanes(pieces, width):
    lane = lanes()
    out = jnp.zeros((8, 128), f32)
    for tile, there, here in pieces:
        moved = tile if there == here else pltpu.roll(tile, (here - there) % 128, 1)
        out = jnp.where((lane >= here) & (lane < here + width), moved, out)
    return out


def inverse(x):
    return jnp.where(x > 0, 1.0 / jnp.where(x > 0, x, 1.0), 0.0)


def split3(x):
    hi = x.astype(bf16).astype(f32)
    rest = x - hi
    mid = rest.astype(bf16).astype(f32)
    return hi, mid, rest - mid


def place_of(p, A, H):
    return (p % A) * H + p // A


def pack_kernel(
    A, H, tok, words, dst, out, norm, beta, mask,
    block, words_v, norm_v, beta_v, mask_v, tok_s, sems,
):
    copies = [
        pltpu.make_async_copy(words, words_v, sems.at[0]),
        pltpu.make_async_copy(norm, norm_v, sems.at[1]),
        pltpu.make_async_copy(beta, beta_v, sems.at[2]),
        pltpu.make_async_copy(mask, mask_v, sems.at[3]),
    ]
    for l in range(A):
        rows = slice(l * CH, (l + 1) * CH)
        copies.append(pltpu.make_async_copy(dst.at[rows], block.at[l, 0:CH], sems.at[4 + 2 * l]))
        copies.append(
            pltpu.make_async_copy(out.at[rows], block.at[l, OUT_AT : OUT_AT + CH], sems.at[5 + 2 * l])
        )
    tok_copy = pltpu.make_async_copy(tok, tok_s, sems.at[4 + 2 * A])
    tok_copy.start()
    for copy in copies:
        copy.start()
    tok_copy.wait()
    vocab = words.shape[0]
    place = lax.axis_index("dst")
    row = lax.broadcasted_iota(jnp.int32, (TB, 1), 0)
    ids = jnp.zeros((TB, 1), jnp.int32)
    for r in range(TB):
        ids = jnp.where(row == r, tok_s[r // TRACES, r % TRACES], ids)
    onehot = jnp.where(lanes((TB, vocab)) == ids - place * vocab, 1.0, 0.0).astype(bf16)
    for copy in copies[:4]:
        copy.wait()
    looked = lax.dot_general(onehot, words_v[...], NN, preferred_element_type=f32)
    looked = jnp.concatenate([looked, jnp.zeros((8, 128), f32)], axis=0).astype(bf16)
    width, RB = mask_v.shape
    for l in range(A):
        block[l, WORD_AT : WORD_AT + 32] = looked
        parts = split3(tiles(beta_v[:, l * CH : (l + 1) * CH]))
        block[l, BETA_AT : BETA_AT + 48] = jnp.concatenate(parts, axis=0).astype(bf16)
        mask_row = mask_v[l // 2 : l // 2 + 1].astype(f32)
        mask_row = jnp.concatenate([mask_row, jnp.zeros((1, 128 - RB), f32)], axis=1)
        norms = split3(norm_v[2 * l : 2 * l + 2])
        block[l, MISC_AT : MISC_AT + 16] = jnp.concatenate(
            [*norms, mask_row, jnp.zeros((9, 128), f32)], axis=0
        ).astype(bf16)
    for copy in copies[4:]:
        copy.wait()


def table_kernel(
    A, H, recv, src_h, table, tops, best, pay, units, count,
    src, src_sem, sums, mass, mask_v, mask_s, word_v, mask_sem,
):
    src_copy = pltpu.make_async_copy(src_h, src, src_sem)
    src_copy.start()
    RB = src.shape[0] // BLK
    for k in range(A):
        misc = recv[k, MISC_AT : MISC_AT + 16].astype(f32)
        mask_v[k : k + 1] = misc[6:7].astype(jnp.int32)
    copy = pltpu.make_async_copy(mask_v, mask_s, mask_sem)
    copy.start()
    tops[...] = jnp.full(tops.shape, very_negative, f32)
    sums[...] = jnp.zeros(sums.shape, f32)
    total = recv[0, WORD_AT : WORD_AT + 32].astype(f32)
    for k in range(1, A):
        total = total + recv[k, WORD_AT : WORD_AT + 32].astype(f32)
    word_v[...] = total
    copy.wait()

    def listing(i, c):
        for k in range(A):
            units[c] = i * A + k
            c = c + mask_s[k, i]
        return c

    cnt = lax.fori_loop(0, RB, listing, 0)
    count[0] = cnt
    src_copy.wait()

    def some(it, carry):
        for q in range(TABLE_UNROLL):
            n = jnp.minimum(it * TABLE_UNROLL + q, cnt - 1)
            u = units[n]
            i = u // A
            k = u - i * A
            cols = recv[k, 0:CH]
            unit_tops, unit_sums = [], []
            for part in range(BLK // 128):
                rows = src[pl.ds(pl.multiple_of(i * BLK + part * 128, 128), 128)]
                scores = lax.dot_general(cols, rows, NT, preferred_element_type=f32)
                top = jnp.max(scores, axis=0, keepdims=True)
                e = jnp.exp(scores - top)
                unit_tops.append(top)
                unit_sums.append(jnp.sum(e, axis=0, keepdims=True))
                table[n, :, part * 128 : (part + 1) * 128] = e.astype(bf16)
            tops[i, pl.ds(k, 1)] = jnp.concatenate(unit_tops, axis=1)
            sums[i, pl.ds(k, 1)] = jnp.concatenate(unit_sums, axis=1)
        return carry

    lax.fori_loop(0, (cnt + TABLE_UNROLL - 1) // TABLE_UNROLL, some, 0)
    for i in range(RB):
        row_best = jnp.max(tops[i], axis=0, keepdims=True)
        best[i : i + 1] = row_best
        mass[i : i + 1] = jnp.sum(sums[i] * jnp.exp(tops[i] - row_best), axis=0, keepdims=True)
    per = TB // A
    mine = lax.axis_index("dst") // H
    words = word_v[pl.ds(mine * per, per)]
    for p in range(2 * RB):
        d = place_of(p, A, H)
        at = (p % 2) * CH
        i = p // 2
        pay[d, 0:1] = best[i : i + 1, at : at + 128]
        pay[d, 1:2] = best[i : i + 1, at + 128 : at + 256]
        pay[d, 2:3] = mass[i : i + 1, at : at + 128]
        pay[d, 3:4] = mass[i : i + 1, at + 128 : at + 256]
        pay[d, 4 : 4 + per] = words
        if pay.shape[1] > 4 + per:
            pay[d, 4 + per :] = jnp.zeros((pay.shape[1] - 4 - per, 128), f32)


def sweep(A, table, units, cnt, unit_work):
    def group(base, size, whole):
        results = []
        for q in range(size):
            n = base + q if whole else jnp.minimum(base + q, cnt - 1)
            u = units[n]
            i = u // A
            k = u - i * A
            results.append((base + q < cnt, unit_work(table[n], i, k)))
        for valid, adds in results:
            for ref, index, value in adds:
                ref[index] += value if whole else jnp.where(valid, value, 0.0)

    def large(it, carry):
        group(it * LARGE, LARGE, True)
        return carry

    whole = cnt // LARGE
    lax.fori_loop(0, whole, large, 0)
    done = whole * LARGE

    def small(it, carry):
        group(done + it * UNROLL, UNROLL, False)
        return carry

    lax.fori_loop(0, (cnt - done + UNROLL - 1) // UNROLL, small, 0)


def backward_unit(weights, factor, acc):
    def work(t, i, k):
        spread = lax.dot_general(weights[k], t, NN, preferred_element_type=f32)
        return [(acc, i, spread * factor(i, k))]

    return work


def halves(x):
    hi = x.astype(bf16)
    return hi, (x - hi.astype(f32)).astype(bf16)


def scatter_rows(pay, acc, A, H, exact=False):
    for p in range(2 * acc.shape[0]):
        part = tiles(acc[p // 2, :, (p % 2) * CH : (p % 2 + 1) * CH])
        d = place_of(p, A, H)
        if exact:
            hi, lo = halves(part)
            pay[d, 0:16] = hi
            pay[d, 16:32] = lo
        else:
            pay[d, 0:16] = part.astype(bf16)


def first_back_kernel(
    A, H, got, recv, tops, best, units, count, table,
    pay, share, emx, em_last, w_last, acc, word_v, em_all,
):
    cnt = count[0]
    D = A * H
    per = TB // A
    for l in range(A):
        total = got[l * H, 4 : 4 + per]
        for h in range(1, H):
            total = total + got[l * H + h, 4 : 4 + per]
        word_v[l * per : (l + 1) * per] = total
    words = word_v[0:TB].astype(bf16)
    top = got[0, 0:2]
    for d in range(1, D):
        top = jnp.maximum(top, got[d, 0:2])
    mass = jnp.zeros_like(top)
    for d in range(D):
        mass = mass + got[d, 2:4] * jnp.exp(got[d, 0:2] - top)
    log_total = top + jnp.log(mass)
    for d in range(D):
        share[d] = jnp.exp(got[d, 0:2] - log_total)
    mine = lax.axis_index("src")
    for k in range(A):
        logits = lax.dot_general(
            words, recv[k, OUT_AT : OUT_AT + CH], NT, preferred_element_type=f32
        )
        misc = recv[k, MISC_AT : MISC_AT + 16].astype(f32)
        norm = misc[0:2] + misc[2:4] + misc[4:6]
        norm = jnp.concatenate([norm[0:1], norm[1:2]], axis=1)
        em = jnp.exp(logits - norm)
        parts = recv[k, BETA_AT : BETA_AT + 48].astype(f32)
        beta = untile(parts[0:16] + parts[16:32] + parts[32:48])
        em_last[k] = em[16:24]
        w_last[k] = (em[16:24] * beta).astype(bf16)
        em_all[k] = em
    emx[...] = em_all[mine]
    acc[...] = jnp.zeros(acc.shape, f32)

    def factor(i, k):
        return jnp.exp(tops[i, pl.ds(k, 1)] - best[pl.ds(i, 1)])

    sweep(A, table, units, cnt, backward_unit(w_last, factor, acc))
    scatter_rows(pay, acc, A, H)
    tail = jnp.concatenate([*split3(log_total), jnp.zeros((10, 128), f32)], axis=0).astype(bf16)
    for d in range(D):
        pay[d, 16:32] = tail


def send_weights(pay, carried, emission, A):
    whole = jnp.sum(carried[0:8] + carried[8:16], axis=1, keepdims=True)
    scaled = tiles(emission * (untile(carried) * inverse(whole))).astype(bf16)
    for k in range(A):
        pay[k, 16:32] = scaled
    return whole


def first_forward_kernel(
    A, H, got, share, alpha, tops, emx, units, count, table,
    pay, factor, acc,
):
    cnt = count[0]
    D = A * H
    RB = tops.shape[0]
    for i in range(RB):
        pieces = []
        for p in (2 * i, 2 * i + 1):
            total = got[place_of(p, A, H), 16:32].astype(f32)
            total = total[0:2] + total[2:4] + total[4:6]
            pieces += [total[0:1], total[1:2]]
        log_total = jnp.concatenate(pieces, axis=1)
        factor[i] = jnp.exp(tops[i] - log_total)
    acc[...] = jnp.zeros(acc.shape, f32)

    def work(t, i, k):
        mix = alpha[:, pl.ds(pl.multiple_of(i * BLK, BLK), BLK)] * factor[i, pl.ds(k, 1)]
        pred = lax.dot_general(mix.astype(bf16), t, NT, preferred_element_type=f32)
        return [(acc, k, pred)]

    sweep(A, table, units, cnt, work)
    for k in range(A):
        pay[k, 0:16] = tiles(acc[k]).astype(pay.dtype)
    first = jnp.zeros((8, 128), f32)
    second = jnp.zeros((8, 128), f32)
    for d in range(D):
        piece = got[d, 0:16].astype(f32)
        first = first + piece[0:8] * share[d, 0:1]
        second = second + piece[8:16] * share[d, 1:2]
    whole = send_weights(pay, jnp.concatenate([first, second], axis=0), emx[8:16], A)
    for k in range(A):
        pay[k, 32:48] = jnp.concatenate(halves(put_lanes([(0, whole)])), axis=0)


def forward_kernel(
    A, H, states, t_at, last, got, factor, w_other, em, held, units, count, table, *rest
):
    if last:
        em_last, terms_in, pay, terms, carried_out, scales, acc, alpha = rest
    else:
        pay, terms, scales, acc, alpha = rest
    cnt = count[0]
    D = A * H
    RB = factor.shape[0]
    at = 32 if last else 16
    total = got[0, at : at + 16].astype(f32)
    for d in range(1, D):
        total = total + got[d, at : at + 16].astype(f32)
    total = total[0:8] + total[8:16]
    rows_sum = jnp.sum(total, axis=1, keepdims=True)
    scale = inverse(rows_sum)
    for p in range(2 * RB):
        u = got[place_of(p, A, H), at : at + 16].astype(f32)
        alpha[p // 2, :, (p % 2) * CH : (p % 2 + 1) * CH] = untile(u) * scale
    acc[...] = jnp.zeros(acc.shape, f32)
    terms[...] = terms_in[...] if last else jnp.zeros(terms.shape, f32)
    lane = lanes()

    def work(t, i, k):
        mix = alpha[i] * factor[i, pl.ds(k, 1)]
        pred = lax.dot_general(mix.astype(bf16), t, NT, preferred_element_type=f32)
        term = jnp.sum(pred * w_other[k].astype(f32), axis=1, keepdims=True)
        return [(acc, k, pred), (terms, k, jnp.where(lane == t_at * RB + i, term, 0.0))]

    sweep(A, table, units, cnt, work)
    if not last:
        for k in range(A):
            pay[k, 0:16] = tiles(acc[k]).astype(pay.dtype)
    spans = [got[d, at + 16 : at + 32].astype(f32) for d in range(D)]
    spans = [x[0:8] + x[8:16] for x in spans]
    cols_sum = spans[0]
    for d in range(1, D):
        cols_sum = cols_sum + spans[d]
    norm = inverse(cols_sum)
    first = jnp.zeros((8, 128), f32)
    second = jnp.zeros((8, 128), f32)
    for d in range(D):
        weight = spans[d] * norm
        piece = got[d, 0:16].astype(f32)
        if last:
            piece = piece + got[d, 16:32].astype(f32)
        first = first + piece[0:8] * weight
        second = second + piece[8:16] * weight
    carried = jnp.concatenate([first, second], axis=0)
    sigma = (held[...] * norm)[:, 0:1]
    if not last:
        whole = send_weights(pay, carried, em[0:8], A)
        for k in range(A):
            pay[k, 32:48] = jnp.concatenate(halves(put_lanes([(0, whole), (1, rows_sum)])), axis=0)
        scales[...] = put_lanes([(0, sigma), (1, rows_sum)])
        return
    carried_out[...] = carried
    products = []
    reach = jnp.zeros((8, 128), f32)
    every = jnp.zeros((8, 128), f32)
    for k in range(A):
        product = (acc[k] * states) * em_last[k]
        products.append((product[:, :128], product[:, 128:]))
        reach = reach + (product[:, :128] + product[:, 128:])
        every = every + terms[k]
    width = CH // A
    for s in range(A):
        at = s * width
        for t in range(2):
            pay[s, t * 8 : t * 8 + 8] = place_lanes(
                [
                    (products[b][at // 128], at % 128, b * width % 128)
                    for b in range(A)
                    if b * width // 128 == t
                ],
                width,
            )
    reach = jnp.sum(reach, axis=1, keepdims=True)
    whole = jnp.sum(first + second, axis=1, keepdims=True)
    ratio_one = em[:, 0:1]
    pairs = []
    for t in range(STEPS):
        here = (lane >= t * RB) & (lane < (t + 1) * RB)
        pairs.append(jnp.sum(jnp.where(here, every, 0.0), axis=1, keepdims=True))
    tail = put_lanes(
        [(0, rows_sum), (1, reach), (2, whole), (3, pairs[0] * sigma), (4, pairs[1] * ratio_one), (5, pairs[2])]
    )
    for k in range(A):
        pay[k, 16:24] = tail
    scales[...] = put_lanes([(0, sigma), (1, ratio_one), (2, rows_sum)])


def back_kernel(
    A, H, states, t_at, got, factor, emx, units, count, table, *rest
):
    if t_at is None:
        pay, weights, held, acc = rest
    else:
        alpha, terms_in, scales_in, pay, terms, ratio, held, acc, weights = rest
    cnt = count[0]
    D = A * H
    RB = factor.shape[0]
    spans = [got[k, 32:48].astype(f32) for k in range(A)]
    spans = [x[0:8] + x[8:16] for x in spans]
    total = spans[0]
    for k in range(1, A):
        total = total + spans[k]
    cols_sum = total[:, 0:1]
    norm = inverse(cols_sum)
    for k in range(A):
        share = spans[k][:, 0:1] * norm
        weights[k] = (untile(got[k, 16:32].astype(f32)) * share).astype(bf16)
    acc[...] = jnp.zeros(acc.shape, f32)
    if t_at is None:
        work = backward_unit(weights, lambda i, k: factor[i, pl.ds(k, 1)], acc)
    else:
        terms[...] = terms_in[...]
        lane = lanes()

        def work(t, i, k):
            spread = lax.dot_general(weights[k], t, NN, preferred_element_type=f32)
            fac = factor[i, pl.ds(k, 1)]
            mix = (alpha[:, pl.ds(pl.multiple_of(i * BLK, BLK), BLK)] * fac).astype(bf16)
            term = jnp.sum(mix.astype(f32) * spread, axis=1, keepdims=True)
            return [
                (acc, i, spread * fac),
                (terms, k, jnp.where(lane == t_at * RB + i, term, 0.0)),
            ]

    sweep(A, table, units, cnt, work)
    scatter_rows(pay, acc, A, H, exact=t_at is not None)
    if t_at is None:
        pred = got[0, 0:16].astype(f32)
        for s in range(1, A):
            pred = pred + got[s, 0:16].astype(f32)
        emission = emx[0:8]
    else:
        inv = inverse(total[:, 1:2])
        pred = jnp.zeros((16, 128), f32)
        for s in range(A):
            weight = spans[s][:, 1:2] * inv * states
            pred = pred + got[s, 0:16].astype(f32) * jnp.concatenate([weight, weight], axis=0)
        emission = emx[8:16]
        rho = scales_in[:, 1:2] * inv
        ratio[...] = put_lanes([(0, rho * scales_in[:, 0:1])])
    product = tiles(untile(pred) * emission).astype(bf16)
    wide = jnp.broadcast_to(cols_sum, (8, 128))
    held[...] = wide
    wide = jnp.concatenate(halves(wide), axis=0)
    at = 16 if t_at is None else 32
    for d in range(D):
        pay[d, at : at + 16] = product
        pay[d, at + 16 : at + 32] = wide


def gather_kernel(A, H, RB, got, carried, terms, scales, pay):
    rows_sum = got[0, 16:24, 0:1]
    for s in range(1, A):
        rows_sum = rows_sum + got[s, 16:24, 0:1]
    inv = inverse(rows_sum)
    pred = jnp.zeros((16, 128), f32)
    tail = jnp.zeros((8, 128), f32)
    lane = lanes()
    for s in range(A):
        share = got[s, 16:24, 0:1] * inv
        pred = pred + got[s, 0:16] * jnp.concatenate([share, share], axis=0)
        piece = got[s, 16:24]
        piece = jnp.where((lane == 1) | (lane == 5), piece * share, piece)
        tail = tail + piece
    tail = jnp.where(lane < 6, tail, 0.0)
    tail = jnp.concatenate([tail[:, 64:], tail[:, :64]], axis=1)
    sigma = scales[:, 0:1]
    one = scales[:, 1:2]
    rho = scales[:, 2:3] * inv
    mult = jnp.where(lane < RB, sigma, jnp.where(lane < 2 * RB, one, jnp.where(lane < 3 * RB, rho, 0.0)))
    width = CH // A
    row, at = alpha_spot(A)
    for k in range(A):
        last = jnp.where(lane < 3 * RB, terms[k] * mult, 0.0) + tail
        there = k * width
        piece = pred[there // 128 * 8 : there // 128 * 8 + 8]
        piece = place_lanes([(piece, there % 128, at)], width)
        for h in range(H):
            if row == 16:
                pay[k * H + h, 16:24] = last + piece
            else:
                pay[k * H + h, 16:24] = last
                pay[k * H + h, row : row + 8] = piece
    back = carried[...]
    for d in range(A * H):
        pay[d, 0:16] = back


def alpha_spot(A):
    width = CH // A
    return (16, 128 - width) if width <= 32 else (24, 0)


def spread_kernel(A, H, got, pay):
    mine = lax.rem(lax.axis_index("dst"), H)
    width = CH // A
    row, at = alpha_spot(A)
    pieces = [got[a * H + mine, row : row + 8] for a in range(A)]
    for t in range(2):
        tile = place_lanes(
            [(pieces[a], at, a * width % 128) for a in range(A) if a * width // 128 == t], width
        )
        for s in range(A):
            pay[s, t * 8 : t * 8 + 8] = tile


def finish_kernel(A, H, states, scale, RB, got, sums, alpha, beta, counts):
    lane = lanes()
    total = got[0, 16:24]
    for d in range(1, A * H):
        total = total + got[d, 16:24]
    for_alpha = states / total[:, 65:66]
    for_beta = states / total[:, 66:67]
    inv = jnp.zeros((8, 128), f32)
    for t in range(STEPS):
        here = (lane >= t * RB) & (lane < (t + 1) * RB)
        inv = jnp.where(here, scale / total[:, 67 + t : 68 + t], inv)
    for p in range(2 * RB):
        beta[:, p * CH : (p + 1) * CH] = untile(got[place_of(p, A, H), 0:16]) * for_beta
    mine = lax.rem(lax.axis_index("dst"), H)
    width = CH // A
    rows = [jnp.zeros((1, 128), f32) for _ in range(counts.shape[0])]
    for l in range(A):
        there = l * width
        for half in range(2):
            value = place_lanes(
                [
                    (sums[s, there // 128 * 8 : there // 128 * 8 + 8], there % 128, s * width % 128)
                    for s in range(A)
                    if s * width // 128 == half
                ],
                width,
            )
            alpha[:, l * CH + half * 128 : l * CH + half * 128 + 128] = value * for_alpha
        line = jnp.where(lane < 3 * RB, got[l * H + mine, 16:24] * inv, 0.0)
        rows[l // 2] = rows[l // 2] + jnp.sum(line, axis=0, keepdims=True)
    out = jnp.concatenate(rows, axis=0)
    counts[...] = out[:, 0:RB] + out[:, RB : 2 * RB] + out[:, 2 * RB : 3 * RB]


def call(body, outs, scratch=(), big=False):
    vm = pl.BlockSpec(memory_space=pltpu.VMEM)
    sm = pl.BlockSpec(memory_space=pltpu.SMEM)
    hbm = pl.BlockSpec(memory_space=pl.ANY)
    kinds = {"v": vm, "s": sm, "h": hbm, "m": vm, "o": vm}
    spaces = {"m": pltpu.VMEM, "h": pltpu.HBM, "o": pltpu.HBM}

    def run(kinds_in, *args):
        return pl.pallas_call(
            body,
            in_specs=[kinds[c] for c in kinds_in],
            out_specs=[kinds[c] for c, _, _ in outs],
            out_shape=[
                spaces[c](s, d) if c in spaces else jax.ShapeDtypeStruct(s, d) for c, s, d in outs
            ],
            scratch_shapes=list(scratch),
            compiler_params=pltpu.CompilerParams(
                vmem_limit_bytes=VMEM_LIMIT if big else 16 * 1024 * 1024
            ),
        )(
            *[
                pltpu.with_memory_space_constraint(a, spaces[c]) if c in spaces else a
                for c, a in zip(kinds_in, args)
            ]
        )

    return run


def local(
    src_emb, dst_emb, out_emb, word_table, log_norm, block_mask, tokens, alpha_start, beta_end
):
    A = lax.axis_size("src")
    D = lax.axis_size("dst")
    H = D // A
    rows = src_emb.shape[0]
    RB = rows // BLK
    states = float(rows * A)
    NB = RB * A
    UN = RB * A
    VM = pltpu.VMEM
    groups = [[h + H * k for k in range(A)] for h in range(H)]
    over_dst = lambda x: lax.all_to_all(x, "dst", 0, 0)
    over_src = lambda x: lax.all_to_all(x, "src", 0, 0)
    part = functools.partial

    (block,) = call(
        part(pack_kernel, A, H),
        [("v", (A, BLOCK_ROWS, 128), bf16)],
        [
            VM(word_table.shape, bf16), VM((dst_emb.shape[0] // 128, 128), f32),
            VM(beta_end.shape, f32), VM(block_mask.shape[::-1], jnp.int32),
            pltpu.SMEM(tokens.shape, jnp.int32), pltpu.SemaphoreType.DMA((5 + 2 * A,)),
        ],
    )(
        "hhhhhhh", tokens, word_table, dst_emb, out_emb,
        log_norm.reshape(-1, 128), beta_end, block_mask.T,
    )
    recv = lax.all_to_all(block, "dst", 0, 0, axis_index_groups=groups)

    per = TB // A
    pay_rows = -(-(4 + per) // 8) * 8
    acc_rows = VM((RB, 8, BLK), f32)
    acc_cols = VM((A, 8, CH), f32)
    table, tops, best, pay, units, count = call(
        part(table_kernel, A, H),
        [
            ("m", (UN, CH, BLK), bf16),
            ("v", (RB, A, BLK), f32),
            ("v", (RB, BLK), f32),
            ("v", (D, pay_rows, 128), f32),
            ("s", (UN,), jnp.int32),
            ("s", (1,), jnp.int32),
        ],
        [
            VM(src_emb.shape, bf16), pltpu.SemaphoreType.DMA(()),
            VM((RB, A, BLK), f32), VM((RB, BLK), f32), VM((A, 128), jnp.int32),
            pltpu.SMEM((A, 128), jnp.int32), VM((32, 128), f32), pltpu.SemaphoreType.DMA(()),
        ],
        big=True,
    )("vh", recv, src_emb)
    got = over_dst(pay)

    pay, share, emx, em_last, w_last = call(
        part(first_back_kernel, A, H),
        [
            ("v", (D, 32, 128), bf16),
            ("v", (D, 2, 128), f32),
            ("v", (TB, CH), f32),
            ("v", (A, 8, CH), f32),
            ("v", (A, 8, CH), bf16),
        ],
        [acc_rows, VM((TB, 128), f32), VM((A, TB, CH), f32)],
        big=True,
    )("vvvvssm", got, recv, tops, best, units, count, table)
    got = over_dst(pay)

    pay, factor = call(
        part(first_forward_kernel, A, H),
        [("v", (A, 48, 128), bf16), ("v", (RB, A, BLK), f32)],
        [acc_cols],
        big=True,
    )("vvvvvssm", got, share, alpha_start, tops, emx, units, count, table)
    got = over_src(pay)

    pay, w_two, held = call(
        part(back_kernel, A, H, states, None),
        [("v", (D, 48, 128), bf16), ("v", (A, 8, CH), bf16), ("v", (8, 128), f32)],
        [acc_rows],
        big=True,
    )("vvvssm", got, factor, emx, units, count, table)
    got = over_dst(pay)

    pay, terms, scales = call(
        part(forward_kernel, A, H, states, 1, False),
        [("v", (A, 48, 128), bf16), ("v", (A, 8, 128), f32), ("v", (8, 128), f32)],
        [acc_cols, acc_rows],
        big=True,
    )("vvvvvssm", got, factor, w_two, emx, held, units, count, table)
    got = over_src(pay)

    pay, terms, ratio, held = call(
        part(back_kernel, A, H, states, 0),
        [
            ("v", (D, 64, 128), bf16), ("v", (A, 8, 128), f32),
            ("v", (8, 128), f32), ("v", (8, 128), f32),
        ],
        [acc_rows, VM((A, 8, CH), bf16)],
        big=True,
    )("vvvssmvvv", got, factor, emx, units, count, table, alpha_start, terms, scales)
    got = over_dst(pay)

    pay, terms, carried, scales = call(
        part(forward_kernel, A, H, states, 2, True),
        [
            ("v", (A, 24, 128), f32), ("v", (A, 8, 128), f32),
            ("v", (16, 128), f32), ("v", (8, 128), f32),
        ],
        [acc_cols, acc_rows],
        big=True,
    )("vvvvvssmvv", got, factor, w_last, ratio, held, units, count, table, em_last, terms)
    got = over_src(pay)

    (pay,) = call(
        part(gather_kernel, A, H, RB), [("v", (D, alpha_spot(A)[0] // 8 * 8 + 8, 128), f32)]
    )("vvvv", got, carried, terms, scales)
    got = over_dst(pay)

    (pay,) = call(part(spread_kernel, A, H), [("v", (A, 16, 128), f32)])("v", got)
    sums = over_src(pay)

    alpha_end, beta_start, counts = call(
        part(finish_kernel, A, H, states, NB * NB / TB, RB),
        [
            ("o", (8, A * CH), f32),
            ("o", (8, rows), f32),
            ("o", (block_mask.shape[1], RB), f32),
        ],
    )("vv", got, sums)
    return (alpha_end, beta_start, counts.T)


def solution(mesh):
    return jax.shard_map(
        local,
        mesh=mesh,
        in_specs=(
            P("src", None),
            P("dst", None),
            P("dst", None),
            P("dst", None),
            P("dst"),
            P("src", "dst"),
            P(),
            P(None, "src"),
            P(None, "dst"),
        ),
        out_specs=(P(None, "dst"), P(None, "src"), P("src", "dst")),
        check_vma=False,
    )
```

```python
import functools

import jax
import jax.numpy as jnp
from jax import lax
from jax.experimental import pallas as pl
from jax.experimental.pallas import tpu as pltpu
from jax.sharding import PartitionSpec as P

BLK = 512
CH = 256
STEPS = 3
TRACES = 8
TB = STEPS * TRACES
UNROLL = 12
LARGE = 24
TABLE_UNROLL = 4
very_negative = -1e30
VMEM_LIMIT = int(20.5 * 1024 * 1024)
NT = (((1,), (1,)), ((), ()))
NN = (((1,), (0,)), ((), ()))
f32 = jnp.float32
bf16 = jnp.bfloat16

OUT_AT = CH
WORD_AT = 2 * CH
BETA_AT = WORD_AT + 32
MISC_AT = BETA_AT + 48
BLOCK_ROWS = MISC_AT + 16


def tiles(x):
    return jnp.concatenate([x[:, :128], x[:, 128:]], axis=0)


def untile(x):
    return jnp.concatenate([x[:8], x[8:16]], axis=1)


def lanes(shape=(8, 128)):
    return lax.broadcasted_iota(jnp.int32, shape, len(shape) - 1)


def put_lanes(pairs):
    lane = lanes()
    out = jnp.zeros((8, 128), f32)
    for at, value in pairs:
        out = jnp.where(lane == at, value, out)
    return out


def place_lanes(pieces, width):
    lane = lanes()
    out = jnp.zeros((8, 128), f32)
    for tile, there, here in pieces:
        moved = tile if there == here else pltpu.roll(tile, (here - there) % 128, 1)
        out = jnp.where((lane >= here) & (lane < here + width), moved, out)
    return out


def inverse(x):
    return jnp.where(x > 0, 1.0 / jnp.where(x > 0, x, 1.0), 0.0)


def split3(x):
    hi = x.astype(bf16).astype(f32)
    rest = x - hi
    mid = rest.astype(bf16).astype(f32)
    return hi, mid, rest - mid


def place_of(p, A, H):
    return (p % A) * H + p // A


def pack_kernel(
    A, H, tok, words, dst, out, norm, beta, mask,
    block, words_v, norm_v, beta_v, mask_v, tok_s, sems,
):
    copies = [
        pltpu.make_async_copy(words, words_v, sems.at[0]),
        pltpu.make_async_copy(norm, norm_v, sems.at[1]),
        pltpu.make_async_copy(beta, beta_v, sems.at[2]),
        pltpu.make_async_copy(mask, mask_v, sems.at[3]),
    ]
    for l in range(A):
        rows = slice(l * CH, (l + 1) * CH)
        copies.append(pltpu.make_async_copy(dst.at[rows], block.at[l, 0:CH], sems.at[4 + 2 * l]))
        copies.append(
            pltpu.make_async_copy(out.at[rows], block.at[l, OUT_AT : OUT_AT + CH], sems.at[5 + 2 * l])
        )
    tok_copy = pltpu.make_async_copy(tok, tok_s, sems.at[4 + 2 * A])
    tok_copy.start()
    for copy in copies:
        copy.start()
    tok_copy.wait()
    vocab = words.shape[0]
    place = lax.axis_index("dst")
    row = lax.broadcasted_iota(jnp.int32, (TB, 1), 0)
    ids = jnp.zeros((TB, 1), jnp.int32)
    for r in range(TB):
        ids = jnp.where(row == r, tok_s[r // TRACES, r % TRACES], ids)
    onehot = jnp.where(lanes((TB, vocab)) == ids - place * vocab, 1.0, 0.0).astype(bf16)
    for copy in copies[:4]:
        copy.wait()
    looked = lax.dot_general(onehot, words_v[...], NN, preferred_element_type=f32)
    looked = jnp.concatenate([looked, jnp.zeros((8, 128), f32)], axis=0).astype(bf16)
    width, RB = mask_v.shape
    for l in range(A):
        block[l, WORD_AT : WORD_AT + 32] = looked
        parts = split3(tiles(beta_v[:, l * CH : (l + 1) * CH]))
        block[l, BETA_AT : BETA_AT + 48] = jnp.concatenate(parts, axis=0).astype(bf16)
        mask_row = mask_v[l // 2 : l // 2 + 1].astype(f32)
        mask_row = jnp.concatenate([mask_row, jnp.zeros((1, 128 - RB), f32)], axis=1)
        norms = split3(norm_v[2 * l : 2 * l + 2])
        block[l, MISC_AT : MISC_AT + 16] = jnp.concatenate(
            [*norms, mask_row, jnp.zeros((9, 128), f32)], axis=0
        ).astype(bf16)
    for copy in copies[4:]:
        copy.wait()


def table_kernel(
    A, H, recv, src_h, table, tops, best, pay, units, count,
    src, src_sem, sums, mass, mask_v, mask_s, word_v, mask_sem,
):
    src_copy = pltpu.make_async_copy(src_h, src, src_sem)
    src_copy.start()
    RB = src.shape[0] // BLK
    for k in range(A):
        misc = recv[k, MISC_AT : MISC_AT + 16].astype(f32)
        mask_v[k : k + 1] = misc[6:7].astype(jnp.int32)
    copy = pltpu.make_async_copy(mask_v, mask_s, mask_sem)
    copy.start()
    tops[...] = jnp.full(tops.shape, very_negative, f32)
    sums[...] = jnp.zeros(sums.shape, f32)
    total = recv[0, WORD_AT : WORD_AT + 32].astype(f32)
    for k in range(1, A):
        total = total + recv[k, WORD_AT : WORD_AT + 32].astype(f32)
    word_v[...] = total
    copy.wait()

    def listing(i, c):
        for k in range(A):
            units[c] = i * A + k
            c = c + mask_s[k, i]
        return c

    cnt = lax.fori_loop(0, RB, listing, 0)
    count[0] = cnt
    src_copy.wait()

    def some(it, carry):
        for q in range(TABLE_UNROLL):
            n = jnp.minimum(it * TABLE_UNROLL + q, cnt - 1)
            u = units[n]
            i = u // A
            k = u - i * A
            cols = recv[k, 0:CH]
            unit_tops, unit_sums = [], []
            for part in range(BLK // 128):
                rows = src[pl.ds(pl.multiple_of(i * BLK + part * 128, 128), 128)]
                scores = lax.dot_general(cols, rows, NT, preferred_element_type=f32)
                top = jnp.max(scores, axis=0, keepdims=True)
                e = jnp.exp(scores - top)
                unit_tops.append(top)
                unit_sums.append(jnp.sum(e, axis=0, keepdims=True))
                table[n, :, part * 128 : (part + 1) * 128] = e.astype(bf16)
            tops[i, pl.ds(k, 1)] = jnp.concatenate(unit_tops, axis=1)
            sums[i, pl.ds(k, 1)] = jnp.concatenate(unit_sums, axis=1)
        return carry

    lax.fori_loop(0, (cnt + TABLE_UNROLL - 1) // TABLE_UNROLL, some, 0)
    for i in range(RB):
        row_best = jnp.max(tops[i], axis=0, keepdims=True)
        best[i : i + 1] = row_best
        mass[i : i + 1] = jnp.sum(sums[i] * jnp.exp(tops[i] - row_best), axis=0, keepdims=True)
    per = TB // A
    mine = lax.axis_index("dst") // H
    words = word_v[pl.ds(mine * per, per)]
    for p in range(2 * RB):
        d = place_of(p, A, H)
        at = (p % 2) * CH
        i = p // 2
        pay[d, 0:1] = best[i : i + 1, at : at + 128]
        pay[d, 1:2] = best[i : i + 1, at + 128 : at + 256]
        pay[d, 2:3] = mass[i : i + 1, at : at + 128]
        pay[d, 3:4] = mass[i : i + 1, at + 128 : at + 256]
        pay[d, 4 : 4 + per] = words
        if pay.shape[1] > 4 + per:
            pay[d, 4 + per :] = jnp.zeros((pay.shape[1] - 4 - per, 128), f32)


def sweep(A, table, units, cnt, unit_work):
    def group(base, size, whole):
        results = []
        for q in range(size):
            n = base + q if whole else jnp.minimum(base + q, cnt - 1)
            u = units[n]
            i = u // A
            k = u - i * A
            results.append((base + q < cnt, unit_work(table[n], i, k)))
        for valid, adds in results:
            for ref, index, value in adds:
                ref[index] += value if whole else jnp.where(valid, value, 0.0)

    def large(it, carry):
        group(it * LARGE, LARGE, True)
        return carry

    whole = cnt // LARGE
    lax.fori_loop(0, whole, large, 0)
    done = whole * LARGE

    def small(it, carry):
        group(done + it * UNROLL, UNROLL, False)
        return carry

    lax.fori_loop(0, (cnt - done + UNROLL - 1) // UNROLL, small, 0)


def backward_unit(weights, factor, acc):
    def work(t, i, k):
        spread = lax.dot_general(weights[k], t, NN, preferred_element_type=f32)
        return [(acc, i, spread * factor(i, k))]

    return work


def halves(x):
    hi = x.astype(bf16)
    return hi, (x - hi.astype(f32)).astype(bf16)


def scatter_rows(pay, acc, A, H, exact=False):
    for p in range(2 * acc.shape[0]):
        part = tiles(acc[p // 2, :, (p % 2) * CH : (p % 2 + 1) * CH])
        d = place_of(p, A, H)
        if exact:
            hi, lo = halves(part)
            pay[d, 0:16] = hi
            pay[d, 16:32] = lo
        else:
            pay[d, 0:16] = part.astype(bf16)


def first_back_kernel(
    A, H, got, recv, tops, best, units, count, table,
    pay, share, emx, em_last, w_last, acc, word_v, em_all,
):
    cnt = count[0]
    D = A * H
    per = TB // A
    for l in range(A):
        total = got[l * H, 4 : 4 + per]
        for h in range(1, H):
            total = total + got[l * H + h, 4 : 4 + per]
        word_v[l * per : (l + 1) * per] = total
    words = word_v[0:TB].astype(bf16)
    top = got[0, 0:2]
    for d in range(1, D):
        top = jnp.maximum(top, got[d, 0:2])
    mass = jnp.zeros_like(top)
    for d in range(D):
        mass = mass + got[d, 2:4] * jnp.exp(got[d, 0:2] - top)
    log_total = top + jnp.log(mass)
    for d in range(D):
        share[d] = jnp.exp(got[d, 0:2] - log_total)
    mine = lax.axis_index("src")
    for k in range(A):
        logits = lax.dot_general(
            words, recv[k, OUT_AT : OUT_AT + CH], NT, preferred_element_type=f32
        )
        misc = recv[k, MISC_AT : MISC_AT + 16].astype(f32)
        norm = misc[0:2] + misc[2:4] + misc[4:6]
        norm = jnp.concatenate([norm[0:1], norm[1:2]], axis=1)
        em = jnp.exp(logits - norm)
        parts = recv[k, BETA_AT : BETA_AT + 48].astype(f32)
        beta = untile(parts[0:16] + parts[16:32] + parts[32:48])
        em_last[k] = em[16:24]
        w_last[k] = (em[16:24] * beta).astype(bf16)
        em_all[k] = em
    emx[...] = em_all[mine]
    acc[...] = jnp.zeros(acc.shape, f32)

    def factor(i, k):
        return jnp.exp(tops[i, pl.ds(k, 1)] - best[pl.ds(i, 1)])

    sweep(A, table, units, cnt, backward_unit(w_last, factor, acc))
    scatter_rows(pay, acc, A, H)
    tail = jnp.concatenate([*split3(log_total), jnp.zeros((10, 128), f32)], axis=0).astype(bf16)
    for d in range(D):
        pay[d, 16:32] = tail


def send_weights(pay, carried, emission, A):
    whole = jnp.sum(carried[0:8] + carried[8:16], axis=1, keepdims=True)
    scaled = tiles(emission * (untile(carried) * inverse(whole))).astype(bf16)
    for k in range(A):
        pay[k, 16:32] = scaled
    return whole


def first_forward_kernel(
    A, H, got, share, alpha, tops, emx, units, count, table,
    pay, factor, acc,
):
    cnt = count[0]
    D = A * H
    RB = tops.shape[0]
    for i in range(RB):
        pieces = []
        for p in (2 * i, 2 * i + 1):
            total = got[place_of(p, A, H), 16:32].astype(f32)
            total = total[0:2] + total[2:4] + total[4:6]
            pieces += [total[0:1], total[1:2]]
        log_total = jnp.concatenate(pieces, axis=1)
        factor[i] = jnp.exp(tops[i] - log_total)
    acc[...] = jnp.zeros(acc.shape, f32)

    def work(t, i, k):
        mix = alpha[:, pl.ds(pl.multiple_of(i * BLK, BLK), BLK)] * factor[i, pl.ds(k, 1)]
        pred = lax.dot_general(mix.astype(bf16), t, NT, preferred_element_type=f32)
        return [(acc, k, pred)]

    sweep(A, table, units, cnt, work)
    for k in range(A):
        pay[k, 0:16] = tiles(acc[k]).astype(pay.dtype)
    first = jnp.zeros((8, 128), f32)
    second = jnp.zeros((8, 128), f32)
    for d in range(D):
        piece = got[d, 0:16].astype(f32)
        first = first + piece[0:8] * share[d, 0:1]
        second = second + piece[8:16] * share[d, 1:2]
    whole = send_weights(pay, jnp.concatenate([first, second], axis=0), emx[8:16], A)
    for k in range(A):
        pay[k, 32:48] = jnp.concatenate(halves(put_lanes([(0, whole)])), axis=0)


def forward_kernel(
    A, H, states, t_at, last, got, factor, w_other, em, held, units, count, table, *rest
):
    if last:
        em_last, terms_in, pay, terms, carried_out, scales, acc, alpha = rest
    else:
        pay, terms, scales, acc, alpha = rest
    cnt = count[0]
    D = A * H
    RB = factor.shape[0]
    at = 32 if last else 16
    total = got[0, at : at + 16].astype(f32)
    for d in range(1, D):
        total = total + got[d, at : at + 16].astype(f32)
    total = total[0:8] + total[8:16]
    rows_sum = jnp.sum(total, axis=1, keepdims=True)
    scale = inverse(rows_sum)
    for p in range(2 * RB):
        u = got[place_of(p, A, H), at : at + 16].astype(f32)
        alpha[p // 2, :, (p % 2) * CH : (p % 2 + 1) * CH] = untile(u) * scale
    acc[...] = jnp.zeros(acc.shape, f32)
    terms[...] = terms_in[...] if last else jnp.zeros(terms.shape, f32)
    lane = lanes()

    def work(t, i, k):
        mix = alpha[i] * factor[i, pl.ds(k, 1)]
        pred = lax.dot_general(mix.astype(bf16), t, NT, preferred_element_type=f32)
        term = jnp.sum(pred * w_other[k].astype(f32), axis=1, keepdims=True)
        return [(acc, k, pred), (terms, k, jnp.where(lane == t_at * RB + i, term, 0.0))]

    sweep(A, table, units, cnt, work)
    if not last:
        for k in range(A):
            pay[k, 0:16] = tiles(acc[k]).astype(pay.dtype)
    spans = [got[d, at + 16 : at + 32].astype(f32) for d in range(D)]
    spans = [x[0:8] + x[8:16] for x in spans]
    cols_sum = spans[0]
    for d in range(1, D):
        cols_sum = cols_sum + spans[d]
    norm = inverse(cols_sum)
    first = jnp.zeros((8, 128), f32)
    second = jnp.zeros((8, 128), f32)
    for d in range(D):
        weight = spans[d] * norm
        piece = got[d, 0:16].astype(f32)
        if last:
            piece = piece + got[d, 16:32].astype(f32)
        first = first + piece[0:8] * weight
        second = second + piece[8:16] * weight
    carried = jnp.concatenate([first, second], axis=0)
    sigma = (held[...] * norm)[:, 0:1]
    if not last:
        whole = send_weights(pay, carried, em[0:8], A)
        for k in range(A):
            pay[k, 32:48] = jnp.concatenate(halves(put_lanes([(0, whole), (1, rows_sum)])), axis=0)
        scales[...] = put_lanes([(0, sigma), (1, rows_sum)])
        return
    carried_out[...] = carried
    products = []
    reach = jnp.zeros((8, 128), f32)
    every = jnp.zeros((8, 128), f32)
    for k in range(A):
        product = (acc[k] * states) * em_last[k]
        products.append((product[:, :128], product[:, 128:]))
        reach = reach + (product[:, :128] + product[:, 128:])
        every = every + terms[k]
    width = CH // A
    for s in range(A):
        at = s * width
        for t in range(2):
            pay[s, t * 8 : t * 8 + 8] = place_lanes(
                [
                    (products[b][at // 128], at % 128, b * width % 128)
                    for b in range(A)
                    if b * width // 128 == t
                ],
                width,
            )
    reach = jnp.sum(reach, axis=1, keepdims=True)
    whole = jnp.sum(first + second, axis=1, keepdims=True)
    ratio_one = em[:, 0:1]
    pairs = []
    for t in range(STEPS):
        here = (lane >= t * RB) & (lane < (t + 1) * RB)
        pairs.append(jnp.sum(jnp.where(here, every, 0.0), axis=1, keepdims=True))
    tail = put_lanes(
        [(0, rows_sum), (1, reach), (2, whole), (3, pairs[0] * sigma), (4, pairs[1] * ratio_one), (5, pairs[2])]
    )
    for k in range(A):
        pay[k, 16:24] = tail
    scales[...] = put_lanes([(0, sigma), (1, ratio_one), (2, rows_sum)])


def back_kernel(
    A, H, states, t_at, got, factor, emx, units, count, table, *rest
):
    if t_at is None:
        pay, weights, held, acc = rest
    else:
        alpha, terms_in, scales_in, pay, terms, ratio, held, acc, weights = rest
    cnt = count[0]
    D = A * H
    RB = factor.shape[0]
    spans = [got[k, 32:48].astype(f32) for k in range(A)]
    spans = [x[0:8] + x[8:16] for x in spans]
    total = spans[0]
    for k in range(1, A):
        total = total + spans[k]
    cols_sum = total[:, 0:1]
    norm = inverse(cols_sum)
    for k in range(A):
        share = spans[k][:, 0:1] * norm
        weights[k] = (untile(got[k, 16:32].astype(f32)) * share).astype(bf16)
    acc[...] = jnp.zeros(acc.shape, f32)
    if t_at is None:
        work = backward_unit(weights, lambda i, k: factor[i, pl.ds(k, 1)], acc)
    else:
        terms[...] = terms_in[...]
        lane = lanes()

        def work(t, i, k):
            spread = lax.dot_general(weights[k], t, NN, preferred_element_type=f32)
            fac = factor[i, pl.ds(k, 1)]
            mix = (alpha[:, pl.ds(pl.multiple_of(i * BLK, BLK), BLK)] * fac).astype(bf16)
            term = jnp.sum(mix.astype(f32) * spread, axis=1, keepdims=True)
            return [
                (acc, i, spread * fac),
                (terms, k, jnp.where(lane == t_at * RB + i, term, 0.0)),
            ]

    sweep(A, table, units, cnt, work)
    scatter_rows(pay, acc, A, H, exact=t_at is not None)
    if t_at is None:
        pred = got[0, 0:16].astype(f32)
        for s in range(1, A):
            pred = pred + got[s, 0:16].astype(f32)
        emission = emx[0:8]
    else:
        inv = inverse(total[:, 1:2])
        pred = jnp.zeros((16, 128), f32)
        for s in range(A):
            weight = spans[s][:, 1:2] * inv * states
            pred = pred + got[s, 0:16].astype(f32) * jnp.concatenate([weight, weight], axis=0)
        emission = emx[8:16]
        rho = scales_in[:, 1:2] * inv
        ratio[...] = put_lanes([(0, rho * scales_in[:, 0:1])])
    product = tiles(untile(pred) * emission).astype(bf16)
    wide = jnp.broadcast_to(cols_sum, (8, 128))
    held[...] = wide
    wide = jnp.concatenate(halves(wide), axis=0)
    at = 16 if t_at is None else 32
    for d in range(D):
        pay[d, at : at + 16] = product
        pay[d, at + 16 : at + 32] = wide


def gather_kernel(A, H, RB, got, carried, terms, scales, pay):
    rows_sum = got[0, 16:24, 0:1]
    for s in range(1, A):
        rows_sum = rows_sum + got[s, 16:24, 0:1]
    inv = inverse(rows_sum)
    pred = jnp.zeros((16, 128), f32)
    tail = jnp.zeros((8, 128), f32)
    lane = lanes()
    for s in range(A):
        share = got[s, 16:24, 0:1] * inv
        pred = pred + got[s, 0:16] * jnp.concatenate([share, share], axis=0)
        piece = got[s, 16:24]
        piece = jnp.where((lane == 1) | (lane == 5), piece * share, piece)
        tail = tail + piece
    tail = jnp.where(lane < 6, tail, 0.0)
    tail = jnp.concatenate([tail[:, 64:], tail[:, :64]], axis=1)
    sigma = scales[:, 0:1]
    one = scales[:, 1:2]
    rho = scales[:, 2:3] * inv
    mult = jnp.where(lane < RB, sigma, jnp.where(lane < 2 * RB, one, jnp.where(lane < 3 * RB, rho, 0.0)))
    width = CH // A
    row, at = alpha_spot(A)
    for k in range(A):
        last = jnp.where(lane < 3 * RB, terms[k] * mult, 0.0) + tail
        there = k * width
        piece = pred[there // 128 * 8 : there // 128 * 8 + 8]
        piece = place_lanes([(piece, there % 128, at)], width)
        for h in range(H):
            if row == 16:
                pay[k * H + h, 16:24] = last + piece
            else:
                pay[k * H + h, 16:24] = last
                pay[k * H + h, row : row + 8] = piece
    back = carried[...]
    for d in range(A * H):
        pay[d, 0:16] = back


def alpha_spot(A):
    width = CH // A
    return (16, 128 - width) if width <= 32 else (24, 0)


def spread_kernel(A, H, got, pay):
    mine = lax.rem(lax.axis_index("dst"), H)
    width = CH // A
    row, at = alpha_spot(A)
    pieces = [got[a * H + mine, row : row + 8] for a in range(A)]
    for t in range(2):
        tile = place_lanes(
            [(pieces[a], at, a * width % 128) for a in range(A) if a * width // 128 == t], width
        )
        for s in range(A):
            pay[s, t * 8 : t * 8 + 8] = tile


def finish_kernel(A, H, states, scale, RB, got, sums, alpha, beta, counts):
    lane = lanes()
    total = got[0, 16:24]
    for d in range(1, A * H):
        total = total + got[d, 16:24]
    for_alpha = states / total[:, 65:66]
    for_beta = states / total[:, 66:67]
    inv = jnp.zeros((8, 128), f32)
    for t in range(STEPS):
        here = (lane >= t * RB) & (lane < (t + 1) * RB)
        inv = jnp.where(here, scale / total[:, 67 + t : 68 + t], inv)
    for p in range(2 * RB):
        beta[:, p * CH : (p + 1) * CH] = untile(got[place_of(p, A, H), 0:16]) * for_beta
    mine = lax.rem(lax.axis_index("dst"), H)
    width = CH // A
    rows = [jnp.zeros((1, 128), f32) for _ in range(counts.shape[0])]
    for l in range(A):
        there = l * width
        for half in range(2):
            value = place_lanes(
                [
                    (sums[s, there // 128 * 8 : there // 128 * 8 + 8], there % 128, s * width % 128)
                    for s in range(A)
                    if s * width // 128 == half
                ],
                width,
            )
            alpha[:, l * CH + half * 128 : l * CH + half * 128 + 128] = value * for_alpha
        line = jnp.where(lane < 3 * RB, got[l * H + mine, 16:24] * inv, 0.0)
        rows[l // 2] = rows[l // 2] + jnp.sum(line, axis=0, keepdims=True)
    out = jnp.concatenate(rows, axis=0)
    counts[...] = out[:, 0:RB] + out[:, RB : 2 * RB] + out[:, 2 * RB : 3 * RB]


def call(body, outs, scratch=(), big=False):
    vm = pl.BlockSpec(memory_space=pltpu.VMEM)
    sm = pl.BlockSpec(memory_space=pltpu.SMEM)
    hbm = pl.BlockSpec(memory_space=pl.ANY)
    kinds = {"v": vm, "s": sm, "h": hbm, "m": vm, "o": vm}
    spaces = {"m": pltpu.VMEM, "h": pltpu.HBM, "o": pltpu.HBM}

    def run(kinds_in, *args):
        return pl.pallas_call(
            body,
            in_specs=[kinds[c] for c in kinds_in],
            out_specs=[kinds[c] for c, _, _ in outs],
            out_shape=[
                spaces[c](s, d) if c in spaces else jax.ShapeDtypeStruct(s, d) for c, s, d in outs
            ],
            scratch_shapes=list(scratch),
            compiler_params=pltpu.CompilerParams(
                vmem_limit_bytes=VMEM_LIMIT if big else 16 * 1024 * 1024
            ),
        )(
            *[
                pltpu.with_memory_space_constraint(a, spaces[c]) if c in spaces else a
                for c, a in zip(kinds_in, args)
            ]
        )

    return run


def local(
    src_emb, dst_emb, out_emb, word_table, log_norm, block_mask, tokens, alpha_start, beta_end
):
    A = lax.axis_size("src")
    D = lax.axis_size("dst")
    H = D // A
    rows = src_emb.shape[0]
    RB = rows // BLK
    states = float(rows * A)
    NB = RB * A
    UN = RB * A
    VM = pltpu.VMEM
    groups = [[h + H * k for k in range(A)] for h in range(H)]
    over_dst = lambda x: lax.all_to_all(x, "dst", 0, 0)
    over_src = lambda x: lax.all_to_all(x, "src", 0, 0)
    part = functools.partial

    (block,) = call(
        part(pack_kernel, A, H),
        [("v", (A, BLOCK_ROWS, 128), bf16)],
        [
            VM(word_table.shape, bf16), VM((dst_emb.shape[0] // 128, 128), f32),
            VM(beta_end.shape, f32), VM(block_mask.shape[::-1], jnp.int32),
            pltpu.SMEM(tokens.shape, jnp.int32), pltpu.SemaphoreType.DMA((5 + 2 * A,)),
        ],
    )(
        "hhhhhhh", tokens, word_table, dst_emb, out_emb,
        log_norm.reshape(-1, 128), beta_end, block_mask.T,
    )
    recv = lax.all_to_all(block, "dst", 0, 0, axis_index_groups=groups)

    per = TB // A
    pay_rows = -(-(4 + per) // 8) * 8
    acc_rows = VM((RB, 8, BLK), f32)
    acc_cols = VM((A, 8, CH), f32)
    table, tops, best, pay, units, count = call(
        part(table_kernel, A, H),
        [
            ("m", (UN, CH, BLK), bf16),
            ("v", (RB, A, BLK), f32),
            ("v", (RB, BLK), f32),
            ("v", (D, pay_rows, 128), f32),
            ("s", (UN,), jnp.int32),
            ("s", (1,), jnp.int32),
        ],
        [
            VM(src_emb.shape, bf16), pltpu.SemaphoreType.DMA(()),
            VM((RB, A, BLK), f32), VM((RB, BLK), f32), VM((A, 128), jnp.int32),
            pltpu.SMEM((A, 128), jnp.int32), VM((32, 128), f32), pltpu.SemaphoreType.DMA(()),
        ],
        big=True,
    )("vh", recv, src_emb)
    got = over_dst(pay)

    pay, share, emx, em_last, w_last = call(
        part(first_back_kernel, A, H),
        [
            ("v", (D, 32, 128), bf16),
            ("v", (D, 2, 128), f32),
            ("v", (TB, CH), f32),
            ("v", (A, 8, CH), f32),
            ("v", (A, 8, CH), bf16),
        ],
        [acc_rows, VM((TB, 128), f32), VM((A, TB, CH), f32)],
        big=True,
    )("vvvvssm", got, recv, tops, best, units, count, table)
    got = over_dst(pay)

    pay, factor = call(
        part(first_forward_kernel, A, H),
        [("v", (A, 48, 128), bf16), ("v", (RB, A, BLK), f32)],
        [acc_cols],
        big=True,
    )("vvvvvssm", got, share, alpha_start, tops, emx, units, count, table)
    got = over_src(pay)

    pay, w_two, held = call(
        part(back_kernel, A, H, states, None),
        [("v", (D, 48, 128), bf16), ("v", (A, 8, CH), bf16), ("v", (8, 128), f32)],
        [acc_rows],
        big=True,
    )("vvvssm", got, factor, emx, units, count, table)
    got = over_dst(pay)

    pay, terms, scales = call(
        part(forward_kernel, A, H, states, 1, False),
        [("v", (A, 48, 128), bf16), ("v", (A, 8, 128), f32), ("v", (8, 128), f32)],
        [acc_cols, acc_rows],
        big=True,
    )("vvvvvssm", got, factor, w_two, emx, held, units, count, table)
    got = over_src(pay)

    pay, terms, ratio, held = call(
        part(back_kernel, A, H, states, 0),
        [
            ("v", (D, 64, 128), bf16), ("v", (A, 8, 128), f32),
            ("v", (8, 128), f32), ("v", (8, 128), f32),
        ],
        [acc_rows, VM((A, 8, CH), bf16)],
        big=True,
    )("vvvssmvvv", got, factor, emx, units, count, table, alpha_start, terms, scales)
    got = over_dst(pay)

    pay, terms, carried, scales = call(
        part(forward_kernel, A, H, states, 2, True),
        [
            ("v", (A, 24, 128), f32), ("v", (A, 8, 128), f32),
            ("v", (16, 128), f32), ("v", (8, 128), f32),
        ],
        [acc_cols, acc_rows],
        big=True,
    )("vvvvvssmvv", got, factor, w_last, ratio, held, units, count, table, em_last, terms)
    got = over_src(pay)

    (pay,) = call(
        part(gather_kernel, A, H, RB), [("v", (D, alpha_spot(A)[0] // 8 * 8 + 8, 128), f32)]
    )("vvvv", got, carried, terms, scales)
    got = over_dst(pay)

    (pay,) = call(part(spread_kernel, A, H), [("v", (A, 16, 128), f32)])("v", got)
    sums = over_src(pay)

    alpha_end, beta_start, counts = call(
        part(finish_kernel, A, H, states, NB * NB / TB, RB),
        [
            ("o", (8, A * CH), f32),
            ("o", (8, rows), f32),
            ("o", (block_mask.shape[1], RB), f32),
        ],
    )("vv", got, sums)
    return (alpha_end, beta_start, counts.T)


def solution(mesh):
    return jax.shard_map(
        local,
        mesh=mesh,
        in_specs=(
            P("src", None),
            P("dst", None),
            P("dst", None),
            P("dst", None),
            P("dst"),
            P("src", "dst"),
            P(),
            P(None, "src"),
            P(None, "dst"),
        ),
        out_specs=(P(None, "dst"), P(None, "src"), P("src", "dst")),
        check_vma=False,
    )
```
